128 devices in a mesh: tile: 8 (over x, core), bulk: 16 (over y, z).
Axes of the slice: x: 4, y: 4, z: 4, core: 2. Of those that a mesh axis runs over, the one named last changes fastest.
Arguments:
- coarse_now: float32 [512, 1024, 128], P('tile', 'bulk'), may hold values from -6 to 6
- coarse_before: float32 [512, 1024, 128], P('tile', 'bulk'), may hold values from -6 to 6
- coarse_courant: float32 [512, 1024, 128], P('tile', 'bulk'), may hold values from 0.05 to 0.3
- coarse_absorb: float32 [512, 1024, 128], P('tile', 'bulk'), may hold values from 0.02 to 0.3
- fine_now: float32 [256, 48, 2304], P(('tile', 'bulk')), may hold values from -6 to 6
- fine_before: float32 [256, 48, 2304], P(('tile', 'bulk')), may hold values from -6 to 6
- fine_courant: float32 [256, 48, 2304], P(('tile', 'bulk')), may hold values from 0.05 to 0.3
- fine_absorb: float32 [256, 48, 2304], P(('tile', 'bulk')), may hold values from 0.02 to 0.3
- box_anchor: int32 [256, 3], P(('tile', 'bulk')), may hold values from 0 to 1008, as said below
- intersection: int32 [128, 4, 4], P(('tile', 'bulk')), may hold values from -1 to 255, as said below
Outputs:
- coarse_next: float32 [512, 1024, 128], P('tile', 'bulk')
- coarse_last: float32 [512, 1024, 128], P('tile', 'bulk')
- fine_next: float32 [256, 48, 2304], P(('tile', 'bulk'))
- fine_last: float32 [256, 48, 2304], P(('tile', 'bulk'))
The draws below stay inside these ranges and needn't reach their ends.
Inputs may be any that keep to these rules, and one draw needn't show every extreme that they name: `box_anchor`: box b is held in the box order of the fine arrays, by device d = b // 2; its region of 16 coarse cells along each dimension from its anchor lies inside the coarse block of device d, d XOR 1, d XOR h or d XOR h XOR 1, where h is half the number of devices; anchors are multiples of 16, and no two regions share a cell. `intersection`: row 0 lists each box exactly once, in the block of the device whose coarse cells hold its region, -1 in unused entries; rows 1 to 3 give that region's first cell relative to the block (0 in unused entries), matching box_anchor. Some block holds exactly 4 boxes.
All inputs are finite; a program needn't handle non-finite values.
Results may differ from the reference program's by a relative error of at most 0.0001.
Values sent between devices are 32-bit elements; how exact they have to be, the bound alone decides.
No kernel may reach another device: no remote copies, remote signals or barrier semaphores. Data moves between devices by JAX's collectives and lax.ppermute only.
A program may use at most 512 MiB of HBM per device.

```python
import math
import jax
import jax.numpy as jnp
from jax import lax

CX = 64
CY = 64
NZ = 128
BC = 16
FINE = 48
BOX_DEV = 2
MOST = 4
STEPS = 2
BOXES = 256
NX = 512
NY = 1024
N_BULK = 16
DEVICES = 128


def layout(key):
    half = DEVICES // 2
    quads = DEVICES // 4
    along_y = CY // BC
    along_z = NZ // BC
    places = CX // BC * along_y * along_z
    first, second, third = jax.random.split(key, 3)
    crowded = jax.random.randint(first, (), 0, quads)
    mirrored = (crowded + 1) % quads
    numbers = jnp.arange(BOXES, dtype=jnp.int32)
    holder = numbers // BOX_DEV
    quad = holder % half // 2
    local = holder % 2 + 2 * (holder // half)
    member = local * BOX_DEV + numbers % BOX_DEV
    orders = jax.vmap(lambda k: jax.random.permutation(k, 4 * MOST))(jax.random.split(second, quads)).astype(jnp.int32)
    picked = orders[quad, member]
    chosen_local = picked // MOST
    chosen_within = picked % MOST
    crowd_local = jnp.where(local % 2 == 0, 1, 0)
    crowd_within = local // 2 * BOX_DEV + numbers % BOX_DEV
    mirror_local = jnp.bitwise_xor(local, 2)
    mirror_within = numbers % BOX_DEV
    target_local = jnp.where(quad == crowded, crowd_local, jnp.where(quad == mirrored, mirror_local, chosen_local))
    within = jnp.where(quad == crowded, crowd_within, jnp.where(quad == mirrored, mirror_within, chosen_within)).astype(jnp.int32)
    block = (2 * quad + target_local % 2 + half * (target_local // 2)).astype(jnp.int32)
    box_slot = (block * MOST + within).astype(jnp.int32)
    rotate = jax.random.randint(third, (DEVICES,), 0, places)
    position = (within + rotate[block]) % places
    offsets = jnp.stack([position // (along_y * along_z) * BC, position // along_z % along_y * BC, position % along_z * BC])
    return (box_slot, block, offsets.astype(jnp.int32))


def draw_box_anchor(key, part):
    box_slot, block, offsets = layout(key)
    first_dim = block // N_BULK * CX + offsets[0]
    second_dim = block % N_BULK * CY + offsets[1]
    return jnp.stack([first_dim, second_dim, offsets[2]], axis=1).astype(jnp.int32)


def draw_intersection(key, part):
    box_slot, block, offsets = layout(key)
    total = DEVICES * MOST
    idents = jnp.full((total,), -1, jnp.int32).at[box_slot].set(jnp.arange(BOXES, dtype=jnp.int32))
    starts = jnp.zeros((3, total), jnp.int32).at[:, box_slot].set(offsets)
    table = jnp.concatenate([idents[None], starts], axis=0)
    return jnp.transpose(table.reshape(4, DEVICES, MOST), (1, 0, 2)).astype(jnp.int32)


def block_levels(own_key, extent, pieces, least, high):
    def one(axis_at, shards_of):
        draws = jax.random.uniform(jax.random.fold_in(jax.random.fold_in(own_key, 6), axis_at), (shards_of,), jnp.float32, least / len(pieces), high / len(pieces))
        return jnp.repeat(jnp.exp(draws), extent[axis_at] // shards_of).reshape((-1,) + (1,) * (len(extent) - axis_at - 1))

    factor_of = one(*pieces[0])
    for cut in pieces[1:]:
        factor_of = factor_of * one(*cut)
    return factor_of


def centred(own_key, dims, spread, bound, shards=(), kind=jnp.bfloat16):
    gain = block_levels(own_key, dims, shards, -0.22, 0.18) if shards else 1.0
    values = jax.random.normal(own_key, dims, jnp.float32) * spread * gain
    return jnp.minimum(jnp.maximum(values, -bound), bound).astype(kind)


def setup_inputs(seed: int = 0) -> dict:
    arg_keys = jax.random.split(jax.random.key(seed), 11)
    return {
        "coarse_now": centred(arg_keys[0], (NX, NY, NZ), 1.0, 6.0, ((0, 8), (1, 16)), jnp.float32),
        "coarse_before": centred(arg_keys[1], (NX, NY, NZ), 1.0, 6.0, ((0, 8), (1, 16)), jnp.float32),
        "coarse_courant": jnp.clip(jnp.exp(math.log(0.3) - 1.7917595 * jax.random.uniform(arg_keys[2], (NX, NY, NZ), jnp.float32) ** block_levels(arg_keys[2], (NX, NY, NZ), ((0, 8), (1, 16)), -0.2, 0.2)), 0.05, 0.3),
        "coarse_absorb": jnp.clip(jnp.exp(math.log(0.3) - 2.7080503 * jax.random.uniform(arg_keys[3], (NX, NY, NZ), jnp.float32) ** block_levels(arg_keys[3], (NX, NY, NZ), ((0, 8), (1, 16)), -0.2, 0.2)), 0.02, 0.3),
        "fine_now": centred(arg_keys[4], (BOXES, FINE, FINE * FINE), 1.0, 6.0, ((0, 128),), jnp.float32),
        "fine_before": centred(arg_keys[5], (BOXES, FINE, FINE * FINE), 1.0, 6.0, ((0, 128),), jnp.float32),
        "fine_courant": jnp.clip(jnp.exp(math.log(0.3) - 1.7917595 * jax.random.uniform(arg_keys[6], (BOXES, FINE, FINE * FINE), jnp.float32) ** block_levels(arg_keys[6], (BOXES, FINE, FINE * FINE), ((0, 128),), -0.2, 0.2)), 0.05, 0.3),
        "fine_absorb": jnp.clip(jnp.exp(math.log(0.3) - 2.7080503 * jax.random.uniform(arg_keys[7], (BOXES, FINE, FINE * FINE), jnp.float32) ** block_levels(arg_keys[7], (BOXES, FINE, FINE * FINE), ((0, 128),), -0.2, 0.2)), 0.02, 0.3),
        "box_anchor": draw_box_anchor(jax.random.fold_in(arg_keys[10], 71), 0),
        "intersection": draw_intersection(jax.random.fold_in(arg_keys[10], 71), 0),
    }


def fine_update(field, before, courant, absorb, ghosts):
    xm = jnp.concatenate([ghosts[0][None], field[:-1]], 0)
    xp = jnp.concatenate([field[1:], ghosts[1][None]], 0)
    ym = jnp.concatenate([ghosts[2][:, None, :], field[:, :-1]], 1)
    yp = jnp.concatenate([field[:, 1:], ghosts[3][:, None, :]], 1)
    zm = jnp.concatenate([ghosts[4][:, :, None], field[:, :, :-1]], 2)
    zp = jnp.concatenate([field[:, :, 1:], ghosts[5][:, :, None]], 2)
    lap = xm + xp + ym + yp + zm + zp - 6.0 * field
    return (2.0 * field - (1.0 - absorb) * before + courant * lap) / (1.0 + absorb)


def upsample(faces):
    return jnp.repeat(jnp.repeat(faces, 3, axis=-2), 3, axis=-1)


def coarse_update(padded, now, before, courant, absorb):
    centre = padded[1:-1, 1:-1, 1:-1]
    beside = padded[2:, 1:-1, 1:-1] + padded[:-2, 1:-1, 1:-1]
    beside = beside + padded[1:-1, 2:, 1:-1] + padded[1:-1, :-2, 1:-1]
    beside = beside + padded[1:-1, 1:-1, 2:] + padded[1:-1, 1:-1, :-2]
    lap = beside - 6.0 * centre
    return (2.0 * now - (1.0 - absorb) * before + courant * lap) / (1.0 + absorb)


def box_faces(padded, start, edge):
    cube = lax.dynamic_slice(padded, (start[0], start[1], start[2]), (edge + 2, edge + 2, edge + 2))
    inner = slice(1, edge + 1)
    return jnp.stack([cube[0, inner, inner], cube[edge + 1, inner, inner], cube[inner, 0, inner], cube[inner, edge + 1, inner], cube[inner, inner, 0], cube[inner, inner, edge + 1]])


def insert_blocks(field, restricted, intersection):
    entries = jnp.transpose(intersection, (0, 2, 1)).reshape(DEVICES * MOST, 4).astype(jnp.int32)
    owners = (jnp.arange(DEVICES * MOST) // MOST).astype(jnp.int32)

    def place_one(index, field):
        row = entries[index]
        device = owners[index]
        ident = row[0]
        safe = jnp.maximum(ident, 0)
        corner = (((device // N_BULK) * CX + row[1]).astype(jnp.int32), ((device % N_BULK) * CY + row[2]).astype(jnp.int32), row[3].astype(jnp.int32))
        current = lax.dynamic_slice(field, corner, (BC, BC, BC))
        block = jnp.where(ident >= 0, restricted[safe], current)
        return lax.dynamic_update_slice(field, block, corner)

    return lax.fori_loop(0, DEVICES * MOST, place_one, field)


def reference(coarse_now, coarse_before, coarse_courant, coarse_absorb, fine_now, fine_before, fine_courant, fine_absorb, box_anchor, intersection):
    shape = (BOXES, FINE, FINE, FINE)
    fine = fine_now.reshape(shape)
    fine_prev = fine_before.reshape(shape)
    fine_c = fine_courant.reshape(shape)
    fine_a = fine_absorb.reshape(shape)
    now = coarse_now
    before = coarse_before
    anchors = box_anchor.astype(jnp.int32)
    faces_all = jax.vmap(box_faces, (None, 0, None))
    for step in range(STEPS):
        padded = jnp.pad(now, 1)
        new = coarse_update(padded, now, before, coarse_courant, coarse_absorb)
        padded_new = jnp.pad(new, 1)
        old_faces = faces_all(padded, anchors, BC)
        new_faces = faces_all(padded_new, anchors, BC)
        for sub in range(3):
            weight = sub / 3.0
            ghosts = upsample(old_faces + weight * (new_faces - old_faces))
            ahead = jax.vmap(fine_update)(fine, fine_prev, fine_c, fine_a, ghosts)
            fine_prev = fine
            fine = ahead
        restricted = fine.reshape(BOXES, BC, 3, BC, 3, BC, 3).mean(axis=(2, 4, 6))
        new = insert_blocks(new, restricted, intersection)
        before = now
        now = new
    flat = (BOXES, FINE, FINE * FINE)
    return now, before, fine.reshape(flat), fine_prev.reshape(flat)
```

```python
import functools

import jax
import jax.numpy as jnp
import numpy as np
from jax import lax
from jax.experimental import pallas as pl
from jax.experimental.pallas import tpu as pltpu
from jax.sharding import PartitionSpec as P

CX = 64
CY = 64
NZ = 128
BC = 16
FINE = 48
PLANE = FINE * FINE
MOST = 4
F32 = jnp.float32
BF16 = jnp.bfloat16
ANY = pl.BlockSpec(memory_space=pl.ANY)
VMEM = pl.BlockSpec(memory_space=pltpu.VMEM)
SMEM = pl.BlockSpec(memory_space=pltpu.SMEM)
LIMIT = 56 * 1024 * 1024


def tables():
    flat = np.arange(PLANE)
    y, z = flat // FINE, flat % FINE
    masks = np.stack([y > 0, y < FINE - 1, z > 0, z < FINE - 1]).astype(np.float32)
    masks = np.repeat(masks[:, None, :], 8, axis=1)
    r = np.arange(BC)[:, None]
    spread = np.zeros((128, PLANE), np.float32)
    spread[0:16] = (y == 0) & (z // 3 == r)
    spread[16:32] = (y == FINE - 1) & (z // 3 == r)
    spread[32:48] = (z == 0) & (y // 3 == r)
    spread[48:64] = (z == FINE - 1) & (y // 3 == r)
    spread[64:80] = z // 3 == r
    spread[80:96] = z // 3 == r
    spread = np.concatenate([spread, spread], axis=0)
    pick = (y // 3 == r).astype(np.float32)
    pool = ((y // 3 * BC + z // 3)[:, None] == np.arange(BC * BC)[None, :]).astype(np.float32)
    return jnp.asarray(masks), jnp.asarray(spread, BF16), jnp.asarray(pick), jnp.asarray(pool, BF16)


def partner_of(meta, device):
    away = (meta[22] * 16 + meta[23]) ^ device
    return (away & 1) + 2 * ((away >> 6) & 1)


def split(value):
    high = value.astype(BF16)
    low = (value - high.astype(F32)).astype(BF16)
    return high, low


def dot(left, right):
    return jnp.dot(left, right, preferred_element_type=F32)


def edges_kernel(p, q, c, a, xup, xdn, yup, ydn, tiles, sem):
    copies = []
    for n, ref in enumerate((p, q, c, a)):
        if n == 0:
            copies.append((ref.at[CX - 2 : CX], xup.at[0:2]))
            copies.append((ref.at[0:2], xdn.at[0:2]))
        else:
            copies.append((ref.at[CX - 1], xup.at[n + 1]))
            copies.append((ref.at[0], xdn.at[n + 1]))
        copies.append((ref.at[:, CY - 8 : CY, :], tiles.at[0, n]))
        copies.append((ref.at[:, 0:8, :], tiles.at[1, n]))
    copies = [pltpu.make_async_copy(*ends, sem.at[n]) for n, ends in enumerate(copies)]
    for copy in copies:
        copy.start()
    for copy in copies:
        copy.wait()
    yup[0:64, :] = tiles[0, 0, :, 6, :]
    yup[64:128, :] = tiles[0, 0, :, 7, :]
    ydn[0:64, :] = tiles[1, 0, :, 0, :]
    ydn[64:128, :] = tiles[1, 0, :, 1, :]
    for n in range(1, 4):
        yup[64 * (n + 1) : 64 * (n + 2), :] = tiles[0, n, :, 7, :]
        ydn[64 * (n + 1) : 64 * (n + 2), :] = tiles[1, n, :, 0, :]
    yup[320:328, :] = jnp.zeros((8, 128), F32)
    ydn[320:328, :] = jnp.zeros((8, 128), F32)


def edges(p, q, c, a):
    x = jax.ShapeDtypeStruct((5, CY, NZ), F32)
    y = jax.ShapeDtypeStruct((5 * CX + 8, NZ), F32)
    return pl.pallas_call(
        edges_kernel,
        out_shape=(x, x, y, y),
        in_specs=[ANY] * 4,
        out_specs=[VMEM] * 4,
        scratch_shapes=[pltpu.VMEM((2, 4, CX, 8, NZ), F32), pltpu.SemaphoreType.DMA((16,))],
        compiler_params=pltpu.CompilerParams(vmem_limit_bytes=LIMIT),
        name="edges",
    )(p, q, c, a)


def corners_kernel(base, meta, yup, ydn, xlo, xhi, yup_out, ydn_out, rows, sem):
    lo = meta[22] > 0
    hi = meta[22] < 7
    for n, y in ((0, CY - 1), (1, 0)):
        rows[n, 0:1, :] = jnp.where(lo, xlo[1, y : y + 1, :], 0.0)
        rows[n, 1:2, :] = jnp.where(hi, xhi[0, y : y + 1, :], 0.0)
    copies = [
        pltpu.make_async_copy(rows.at[0], yup_out.at[base : base + 8, :], sem.at[0]),
        pltpu.make_async_copy(rows.at[1], ydn_out.at[base : base + 8, :], sem.at[1]),
    ]
    for copy in copies:
        copy.start()
    for copy in copies:
        copy.wait()


def corners(meta, yup, ydn, xlo, xhi):
    base = yup.shape[0] - 8
    y = jax.ShapeDtypeStruct(yup.shape, F32)
    return pl.pallas_call(
        functools.partial(corners_kernel, base),
        out_shape=(y, y),
        in_specs=[SMEM, ANY, ANY, VMEM, VMEM],
        out_specs=[ANY, ANY],
        input_output_aliases={1: 0, 2: 1},
        scratch_shapes=[pltpu.VMEM((2, 8, NZ), F32), pltpu.SemaphoreType.DMA((2,))],
        compiler_params=pltpu.CompilerParams(vmem_limit_bytes=LIMIT),
        name="corners",
    )(meta, yup, ydn, xlo, xhi)


def coarse_kernel(
    first,
    meta,
    p,
    q,
    c,
    a,
    pxlo,
    pxhi,
    pylo,
    pyhi,
    exlo,
    exhi,
    eylo,
    eyhi,
    new_out,
    face0,
    face1,
    face2,
    face3,
    pe,
    ne,
    ring,
    faces,
    sem,
):
    load = pltpu.make_async_copy(p, pe.at[2 : CX + 2, 8 : CY + 8, :], sem.at[0])
    load.start()
    tile, bulk = meta[22], meta[23]
    has = {"xl": tile > 0, "xh": tile < 7, "yl": bulk > 0, "yh": bulk < 15}
    base = pylo.shape[0] - 8
    qlo, qhi = (2, 2) if first else (1, 0)

    def keep(side, value):
        return jnp.where(has[side], value, 0.0)

    pe[0, 8 : CY + 8, :] = keep("xl", pxlo[0])
    pe[1, 8 : CY + 8, :] = keep("xl", pxlo[1])
    pe[CX + 2, 8 : CY + 8, :] = keep("xh", pxhi[0])
    pe[CX + 3, 8 : CY + 8, :] = keep("xh", pxhi[1])
    lo_edge = keep("yl", pylo[64:128, :])
    hi_edge = keep("yh", pyhi[0:64, :])
    pe[2 : CX + 2, 7:8, :] = lo_edge[:, None, :]
    pe[2 : CX + 2, CY + 8 : CY + 9, :] = hi_edge[:, None, :]
    pe[1, 7:8, :] = keep("yl", pylo[base : base + 1, :])
    pe[CX + 2, 7:8, :] = keep("yl", pylo[base + 1 : base + 2, :])
    pe[1, CY + 8 : CY + 9, :] = keep("yh", pyhi[base : base + 1, :])
    pe[CX + 2, CY + 8 : CY + 9, :] = keep("yh", pyhi[base + 1 : base + 2, :])
    load.wait()

    lane = lax.broadcasted_iota(jnp.int32, (64, NZ), 1)
    inner_lo, inner_hi = lane > 0, lane < NZ - 1

    def along_z(here):
        return jnp.where(inner_lo, pltpu.roll(here, 1, 1), 0.0) + jnp.where(
            inner_hi, pltpu.roll(here, NZ - 1, 1), 0.0
        )

    def step(here, beside, before, courant, absorb):
        inv = 1.0 / (1.0 + absorb)
        return before + (2.0 * inv) * (here - before) + (courant * inv) * (beside - 6.0 * here)

    def row(i, before, courant, absorb):
        here = pe[i, 8 : CY + 8, :]
        beside = pe[i - 1, 8 : CY + 8, :] + pe[i + 1, 8 : CY + 8, :]
        beside = beside + pe[i, 7 : CY + 7, :] + pe[i, 9 : CY + 9, :] + along_z(here)
        return step(here, beside, before, courant, absorb)

    def body(x, carry):
        ne[x + 1, 8 : CY + 8, :] = row(x + 2, q[x], c[x], a[x])
        return carry

    lax.fori_loop(0, CX, body, 0, unroll=2)
    store = pltpu.make_async_copy(ne.at[1 : CX + 1, 8 : CY + 8, :], new_out, sem.at[1])
    store.start()

    ne[0, 8 : CY + 8, :] = row(1, keep("xl", exlo[qlo]), keep("xl", exlo[3]), keep("xl", exlo[4]))
    ne[CX + 1, 8 : CY + 8, :] = row(
        CX + 2, keep("xh", exhi[qhi]), keep("xh", exhi[3]), keep("xh", exhi[4])
    )

    def side(name, here, out, inside, first_corner, last_corner, extra, at_q):
        ring[7:8, :] = keep(name, first_corner)
        ring[8:72, :] = here
        ring[72:73, :] = keep(name, last_corner)
        beside = ring[7:71, :] + ring[9:73, :] + out + inside + along_z(here)
        part = [keep(name, extra[64 * n : 64 * n + 64, :]) for n in (at_q, 3, 4)]
        return step(here, beside, *part)

    inside = pe[2 : CX + 2, 8, :]
    out = keep("yl", pylo[0:64, :])
    value = side(
        "yl", lo_edge, out, inside, pylo[base : base + 1, :], pylo[base + 1 : base + 2, :], eylo, qlo
    )
    ne[1 : CX + 1, 7:8, :] = value[:, None, :]
    inside = pe[2 : CX + 2, CY + 7, :]
    out = keep("yh", pyhi[64:128, :])
    value = side(
        "yh", hi_edge, out, inside, pyhi[base : base + 1, :], pyhi[base + 1 : base + 2, :], eyhi, qhi
    )
    ne[1 : CX + 1, CY + 8 : CY + 9, :] = value[:, None, :]

    from_z = lax.broadcasted_iota(jnp.int32, (NZ, NZ), 0)
    to_lane = lax.broadcasted_iota(jnp.int32, (NZ, NZ), 1)
    out_lane = lax.broadcasted_iota(jnp.int32, (BC, NZ), 1)
    deep_lane = lax.broadcasted_iota(jnp.int32, (BC, BC, NZ), 2)
    deep_y = lax.broadcasted_iota(jnp.int32, (BC, BC, NZ), 1)
    diagonal = (deep_lane & 15) == deep_y

    def entry(k, carry):
        ident = meta[k]

        @pl.when(ident >= 0)
        def _():
            ox = meta[4 + k]
            oy = pl.multiple_of(meta[8 + k], 16)
            oz = meta[12 + k]
            where_to = partner_of(meta, ident >> 1) * 2 + (ident & 1)
            low_face = (to_lane >= 32) & (to_lane < 48)
            high_face = (to_lane >= 48) & (to_lane < 64)
            source = jnp.where(
                low_face, oz - 1, jnp.where(high_face, oz + BC, oz + (to_lane & 15))
            )
            mover = jnp.where(from_z == source, 1.0, 0.0).astype(BF16)
            mover = jnp.concatenate([mover, mover], axis=0)
            for t, (ref, off) in enumerate(((pe, 2), (ne, 1))):
                cube = ref[pl.ds(ox + off, BC), pl.ds(oy + 8, BC), :].reshape(BC * BC, NZ)
                ym = ref[pl.ds(ox + off, BC), pl.ds(oy, 8), :][:, 7, :]
                yp = ref[pl.ds(ox + off, BC), pl.ds(oy + 8 + BC, 8), :][:, 0, :]
                xm = ref[ox + off - 1, pl.ds(oy + 8, BC), :]
                xp = ref[ox + off + BC, pl.ds(oy + 8, BC), :]
                high, low = split(jnp.concatenate([cube, ym, yp, xm, xp], axis=0))
                moved = dot(jnp.concatenate([high, low], axis=1), mover)
                z_face = jnp.where(diagonal, moved[0:256].reshape(BC, BC, NZ), 0.0).sum(axis=1)
                tile_ = jnp.where(out_lane < 80, moved[288:304], moved[304:320])
                tile_ = jnp.where(out_lane < 64, z_face, tile_)
                tile_ = jnp.where(out_lane < 32, moved[272:288], tile_)
                tile_ = jnp.where(out_lane < 16, moved[256:272], tile_)
                faces[where_to, t] = tile_

        return carry

    lax.fori_loop(0, MOST, entry, 0)
    for n, ref in enumerate((face0, face1, face2, face3)):
        ref[...] = faces[2 * n : 2 * n + 2]
    store.wait()


def coarse(first, meta, p, q, c, a, halos, extras):
    face = jax.ShapeDtypeStruct((2, 2, BC, NZ), F32)
    return pl.pallas_call(
        functools.partial(coarse_kernel, first),
        out_shape=(jax.ShapeDtypeStruct((CX, CY, NZ), F32), face, face, face, face),
        in_specs=[SMEM, ANY] + [VMEM] * 11,
        out_specs=[ANY] + [VMEM] * 4,
        scratch_shapes=[
            pltpu.VMEM((CX + 4, CY + 16, NZ), F32),
            pltpu.VMEM((CX + 2, CY + 16, NZ), F32),
            pltpu.VMEM((80, NZ), F32),
            pltpu.VMEM((8, 2, BC, NZ), F32),
            pltpu.SemaphoreType.DMA((2,)),
        ],
        compiler_params=pltpu.CompilerParams(vmem_limit_bytes=LIMIT),
        name="coarse",
    )(meta, p, q, c, a, *halos, *extras)


def fine_kernel(
    meta,
    f,
    g,
    c,
    a,
    r0,
    r1,
    r2,
    r3,
    masks,
    spread,
    pick,
    pool,
    f_out,
    g_out,
    res,
    buf,
    two,
    cour,
    ghost,
    delta,
    xrow,
    faces,
    sem,
):
    copies = [
        pltpu.make_async_copy(f, buf.at[0, :, 8:56, :], sem.at[0]),
        pltpu.make_async_copy(g, buf.at[1, :, 8:56, :], sem.at[1]),
    ]
    for copy in copies:
        copy.start()
    for n, ref in enumerate((r0, r1, r2, r3)):
        faces[2 * n : 2 * n + 2] = ref[...]

    lane = lax.broadcasted_iota(jnp.int32, (BC, NZ), 1)
    tall = lax.broadcasted_iota(jnp.int32, (FINE, BC), 0)
    wide = lax.broadcasted_iota(jnp.int32, (FINE, BC), 1)
    thrice = jnp.where((tall >= 3 * wide) & (tall < 3 * wide + 3), 1.0, 0.0).astype(BF16)
    for j in range(2):
        source = (meta[16 + 3 * j] >> 6) * 16 + (meta[17 + 3 * j] >> 6)
        at = partner_of(meta, source) * 2 + j
        sides, rows = [], []
        for t in range(2):
            got = faces[at, t]
            high, low = split(jnp.where(lane < 96, got, 0.0))
            both = jnp.concatenate([high, low], axis=1)
            wide_lane = jnp.concatenate([lane, lane], axis=1)
            zero = jnp.zeros_like(both)
            sides.append(dot(thrice, jnp.where(wide_lane < 64, both, zero)).astype(BF16))
            rows.append(jnp.where((wide_lane >= 64) & (wide_lane < 80), both, zero))
            rows.append(jnp.where(wide_lane >= 80, both, zero))
        spreaded = dot(jnp.concatenate(sides + rows, axis=0), spread[...])
        ghost[j] = spreaded[0:48]
        delta[j] = spreaded[48:96] - spreaded[0:48]
        for n in range(4):
            part = spreaded[96 + 16 * n : 112 + 16 * n] * pick[...]
            xrow[j, n : n + 1, :] = part.sum(axis=0, keepdims=True)
        for i in range(6):
            s = slice(8 * i, 8 * i + 8)
            inv = 1.0 / (1.0 + a[j, s, :])
            two[j, s, :] = 2.0 * inv
            cour[j, s, :] = c[j, s, :] * inv
    for copy in copies:
        copy.wait()

    tiles = PLANE // 128
    small = lax.broadcasted_iota(jnp.int32, (8, 128), 1)
    from_before = {1: small < 1, 48: small < 48}
    from_after = {1: small >= 127, 48: small >= 80}

    def substep(m, j):
        now, old = m % 2, 1 - m % 2
        weight = m / 3.0
        for n, at in ((0, 7), (1, 56)):
            first = xrow[j, n : n + 1, :]
            last = xrow[j, n + 2 : n + 3, :]
            buf[now, j, at : at + 1, :] = first + weight * (last - first)
        for i in range(6):
            s = slice(8 * i, 8 * i + 8)

            def here(k):
                return buf[now, j, 8 + 8 * i : 16 + 8 * i, 128 * k : 128 * k + 128]

            def turned(v):
                return {d: (pltpu.roll(v, d, 1), pltpu.roll(v, 128 - d, 1)) for d in (1, 48)}

            cur = here(0)
            cur_t = turned(cur)
            before_t = cur_t
            for k in range(tiles):
                ls = slice(128 * k, 128 * k + 128)
                nxt = here(k + 1) if k + 1 < tiles else cur
                nxt_t = turned(nxt) if k + 1 < tiles else cur_t
                total = (
                    buf[now, j, 7 + 8 * i : 15 + 8 * i, ls] + buf[now, j, 9 + 8 * i : 17 + 8 * i, ls]
                )
                for d, n in ((48, 0), (1, 2)):
                    down = jnp.where(from_before[d], before_t[d][0], cur_t[d][0])
                    up = jnp.where(from_after[d], nxt_t[d][1], cur_t[d][1])
                    total = total + down * masks[n, :, ls] + up * masks[n + 1, :, ls]
                edge = ghost[j, s, ls]
                if m > 0:
                    edge = edge + weight * delta[j, s, ls]
                total = total + edge - 6.0 * cur
                prev = buf[old, j, 8 + 8 * i : 16 + 8 * i, ls]
                buf[old, j, 8 + 8 * i : 16 + 8 * i, ls] = (
                    prev + two[j, s, ls] * (cur - prev) + cour[j, s, ls] * total
                )
                before_t, cur, cur_t = cur_t, nxt, nxt_t

    def box(j, carry):
        for m in range(3):
            substep(m, j)
        return carry

    lax.fori_loop(0, 2, box, 0)
    stores = [
        pltpu.make_async_copy(buf.at[1, :, 8:56, :], f_out, sem.at[0]),
        pltpu.make_async_copy(buf.at[0, :, 8:56, :], g_out, sem.at[1]),
    ]
    for copy in stores:
        copy.start()
    tall = lax.broadcasted_iota(jnp.int32, (BC, FINE), 1)
    wide = lax.broadcasted_iota(jnp.int32, (BC, FINE), 0)
    gather = jnp.where((tall >= 3 * wide) & (tall < 3 * wide + 3), 1.0, 0.0).astype(BF16)
    for j in range(2):
        high, low = split(buf[1, j, 8:56, :])
        pooled = dot(high, pool[...]) + dot(low, pool[...])
        high, low = split(pooled)
        res[j] = (dot(gather, high) + dot(gather, low)) * (1.0 / 27.0)
    for copy in stores:
        copy.wait()


def fine(meta, f, g, c, a, received, consts):
    box = jax.ShapeDtypeStruct((2, FINE, PLANE), F32)
    return pl.pallas_call(
        fine_kernel,
        out_shape=(box, box, jax.ShapeDtypeStruct((2, BC, BC * BC), F32)),
        in_specs=[SMEM, ANY, ANY] + [VMEM] * 10,
        out_specs=[ANY, ANY, VMEM],
        scratch_shapes=[
            pltpu.VMEM((2, 2, 64, PLANE), F32),
            pltpu.VMEM((2, FINE, PLANE), F32),
            pltpu.VMEM((2, FINE, PLANE), F32),
            pltpu.VMEM((2, FINE, PLANE), F32),
            pltpu.VMEM((2, FINE, PLANE), F32),
            pltpu.VMEM((2, 8, PLANE), F32),
            pltpu.VMEM((8, 2, BC, NZ), F32),
            pltpu.SemaphoreType.DMA((2,)),
        ],
        compiler_params=pltpu.CompilerParams(vmem_limit_bytes=LIMIT),
        name="fine",
    )(meta, f, g, c, a, *received, *consts)


def insert_kernel(pack, meta, new, r0, r1, r2, r3, out, *rest):
    if pack:
        xup, xdn, yup, ydn, got, sem = rest
    else:
        got, sem = rest
    load = pltpu.make_async_copy(new, out, sem)
    load.start()
    for n, ref in enumerate((r0, r1, r2, r3)):
        got[2 * n : 2 * n + 2] = ref[...]
    load.wait()
    y_of = lax.broadcasted_iota(jnp.int32, (BC, BC, BC * BC), 1)
    lane_of = lax.broadcasted_iota(jnp.int32, (BC, BC, BC * BC), 2)
    mine = (lane_of >> 4) == y_of
    from_yz = lax.broadcasted_iota(jnp.int32, (BC * BC, NZ), 0)
    to_lane = lax.broadcasted_iota(jnp.int32, (BC * BC, NZ), 1)
    lane = lax.broadcasted_iota(jnp.int32, (BC, BC, NZ), 2)

    def entry(k, carry):
        ident = meta[k]

        @pl.when(ident >= 0)
        def _():
            ox = meta[4 + k]
            oy = pl.multiple_of(meta[8 + k], 16)
            oz = meta[12 + k]
            value = got[partner_of(meta, ident >> 1) * 2 + (ident & 1)]
            full = jnp.where(mine, value[:, None, :], 0.0).reshape(BC * BC, BC * BC)
            high, low = split(full)
            mover = jnp.where(to_lane == oz + (from_yz & 15), 1.0, 0.0).astype(BF16)
            moved = (dot(high, mover) + dot(low, mover)).reshape(BC, BC, NZ)
            current = out[pl.ds(ox, BC), pl.ds(oy, BC), :]
            out[pl.ds(ox, BC), pl.ds(oy, BC), :] = jnp.where(
                (lane >= oz) & (lane < oz + BC), moved, current
            )

        return carry

    lax.fori_loop(0, MOST, entry, 0)
    if pack:
        xup[...] = out[CX - 2 : CX]
        xdn[...] = out[0:2]
        yup[0:64, :] = out[:, CY - 2, :]
        yup[64:128, :] = out[:, CY - 1, :]
        ydn[0:64, :] = out[:, 0, :]
        ydn[64:128, :] = out[:, 1, :]
        yup[128:136, :] = jnp.zeros((8, NZ), F32)
        ydn[128:136, :] = jnp.zeros((8, NZ), F32)


def insert(pack, meta, new, received):
    shapes = [jax.ShapeDtypeStruct((CX, CY, NZ), F32)]
    if pack:
        x = jax.ShapeDtypeStruct((2, CY, NZ), F32)
        y = jax.ShapeDtypeStruct((2 * CX + 8, NZ), F32)
        shapes += [x, x, y, y]
    return pl.pallas_call(
        functools.partial(insert_kernel, pack),
        out_shape=tuple(shapes),
        in_specs=[SMEM, ANY] + [VMEM] * 4,
        out_specs=[VMEM] * len(shapes),
        scratch_shapes=[pltpu.VMEM((8, BC, BC * BC), F32), pltpu.SemaphoreType.DMA],
        compiler_params=pltpu.CompilerParams(vmem_limit_bytes=LIMIT),
        name="insert",
    )(meta, new, *received)


def ring(size, by):
    return [(i, (i + by) % size) for i in range(size)]


def halo(meta, xup, xdn, yup, ydn):
    xlo = lax.ppermute(xup, "tile", ring(8, 1))
    xhi = lax.ppermute(xdn, "tile", ring(8, -1))
    yup, ydn = corners(meta, yup, ydn, xlo, xhi)
    ylo = lax.ppermute(yup, "bulk", ring(16, 1))
    yhi = lax.ppermute(ydn, "bulk", ring(16, -1))
    return xlo, xhi, ylo, yhi


def trade(values):
    done = [values[0]]
    for value, away in zip(values[1:], (1, 64, 65)):
        done.append(lax.ppermute(value, ("tile", "bulk"), [(d, d ^ away) for d in range(128)]))
    return done


def on_device(
    coarse_now,
    coarse_before,
    coarse_courant,
    coarse_absorb,
    fine_now,
    fine_before,
    fine_courant,
    fine_absorb,
    box_anchor,
    intersection,
):
    place = jnp.stack([lax.axis_index("tile"), lax.axis_index("bulk")]).astype(jnp.int32)
    meta = jnp.concatenate([intersection.reshape(16), box_anchor.reshape(6), place])
    consts = tables()
    extras = halo(meta, *edges(coarse_now, coarse_before, coarse_courant, coarse_absorb))
    halos = extras
    p, q = coarse_now, coarse_before
    f, g = fine_now, fine_before
    for step in range(2):
        new, *faces = coarse(
            step == 0, meta, p, q, coarse_courant, coarse_absorb, halos, extras
        )
        f, g, res = fine(meta, f, g, fine_courant, fine_absorb, trade(faces), consts)
        back = trade([res] * 4)
        if step == 0:
            new, *packed = insert(True, meta, new, back)
            halos = halo(meta, *packed)
        else:
            (new,) = insert(False, meta, new, back)
        p, q = new, p
    return p, q, f, g


def solution(mesh):
    grid = P("tile", "bulk", None)
    boxes = P(("tile", "bulk"), None, None)
    in_specs = (grid,) * 4 + (boxes,) * 4 + (P(("tile", "bulk"), None), boxes)
    return jax.shard_map(
        on_device, mesh=mesh, in_specs=in_specs, out_specs=(grid, grid, boxes, boxes), check_vma=False
    )
```

```python
import functools

import jax
import jax.numpy as jnp
import numpy as np
from jax import lax
from jax.experimental import pallas as pl
from jax.experimental.pallas import tpu as pltpu
from jax.sharding import PartitionSpec as P

CX = 64
CY = 64
NZ = 128
BC = 16
FINE = 48
PLANE = FINE * FINE
MOST = 4
F32 = jnp.float32
BF16 = jnp.bfloat16
ANY = pl.BlockSpec(memory_space=pl.ANY)
HBM = pl.BlockSpec(memory_space=pltpu.HBM)
VMEM = pl.BlockSpec(memory_space=pltpu.VMEM)
SMEM = pl.BlockSpec(memory_space=pltpu.SMEM)
LIMIT = 20 * 1024 * 1024


def tables():
    flat = np.arange(PLANE)
    y, z = flat // FINE, flat % FINE
    masks = np.stack([z > 0, z < FINE - 1]).astype(np.float32)
    masks = np.repeat(masks[:, None, :], 8, axis=1)
    r = np.arange(BC)[:, None]
    spread = np.zeros((128, PLANE), np.float32)
    spread[0:16] = (y == 0) & (z // 3 == r)
    spread[16:32] = (y == FINE - 1) & (z // 3 == r)
    spread[32:48] = (z == 0) & (y // 3 == r)
    spread[48:64] = (z == FINE - 1) & (y // 3 == r)
    spread[64:80] = z // 3 == r
    spread[80:96] = z // 3 == r
    spread = np.concatenate([spread, spread], axis=0)
    pick = (y // 3 == r).astype(np.float32)
    pool = ((y // 3 * BC + z // 3)[:, None] == np.arange(BC * BC)[None, :]).astype(np.float32)
    return jnp.asarray(masks), jnp.asarray(spread, BF16), jnp.asarray(pick), jnp.asarray(pool, BF16)


def partner_of(meta, device):
    away = (meta[22] * 16 + meta[23]) ^ device
    return (away & 1) + 2 * ((away >> 6) & 1)


def far(value):
    return pltpu.with_memory_space_constraint(value, pltpu.HBM)


def split(value):
    high = value.astype(BF16)
    low = (value - high.astype(F32)).astype(BF16)
    return high, low


def dot(left, right):
    return jnp.dot(left, right, preferred_element_type=F32)


def edges_kernel(p, q, c, a, xup, xdn, yup, ydn, tiles, sem):
    copies = []
    for n, ref in enumerate((p, q, c, a)):
        if n == 0:
            copies.append((ref.at[CX - 2 : CX], xup.at[0:2]))
            copies.append((ref.at[0:2], xdn.at[0:2]))
        else:
            copies.append((ref.at[CX - 1], xup.at[n + 1]))
            copies.append((ref.at[0], xdn.at[n + 1]))
        copies.append((ref.at[:, CY - 8 : CY, :], tiles.at[0, n]))
        copies.append((ref.at[:, 0:8, :], tiles.at[1, n]))
    copies = [pltpu.make_async_copy(*ends, sem.at[n]) for n, ends in enumerate(copies)]
    for copy in copies:
        copy.start()
    for copy in copies:
        copy.wait()

    def plane(side, n, y):
        return tiles.at[side, n].reshape(CX * 8, NZ)[pl.ds(y, CX, stride=8), :]

    yup[0:64, :] = plane(0, 0, 6)
    yup[64:128, :] = plane(0, 0, 7)
    ydn[0:64, :] = plane(1, 0, 0)
    ydn[64:128, :] = plane(1, 0, 1)
    for n in range(1, 4):
        yup[64 * (n + 1) : 64 * (n + 2), :] = plane(0, n, 7)
        ydn[64 * (n + 1) : 64 * (n + 2), :] = plane(1, n, 0)
    yup[320:328, :] = jnp.zeros((8, 128), F32)
    ydn[320:328, :] = jnp.zeros((8, 128), F32)


def edges(p, q, c, a):
    x = jax.ShapeDtypeStruct((5, CY, NZ), F32)
    y = jax.ShapeDtypeStruct((5 * CX + 8, NZ), F32)
    return pl.pallas_call(
        edges_kernel,
        out_shape=(x, x, y, y),
        in_specs=[HBM] * 4,
        out_specs=[VMEM] * 4,
        scratch_shapes=[pltpu.VMEM((2, 4, CX, 8, NZ), F32), pltpu.SemaphoreType.DMA((16,))],
        compiler_params=pltpu.CompilerParams(vmem_limit_bytes=LIMIT),
        name="edges",
    )(*[far(v) for v in (p, q, c, a)])


def corners_kernel(base, meta, yup, ydn, xlo, xhi, yup_out, ydn_out, rows, sem):
    lo = meta[22] > 0
    hi = meta[22] < 7
    for n, y in ((0, CY - 1), (1, 0)):
        rows[n, 0:1, :] = jnp.where(lo, xlo[1, y : y + 1, :], 0.0)
        rows[n, 1:2, :] = jnp.where(hi, xhi[0, y : y + 1, :], 0.0)
    copies = [
        pltpu.make_async_copy(rows.at[0], yup_out.at[base : base + 8, :], sem.at[0]),
        pltpu.make_async_copy(rows.at[1], ydn_out.at[base : base + 8, :], sem.at[1]),
    ]
    for copy in copies:
        copy.start()
    for copy in copies:
        copy.wait()


def corners(meta, yup, ydn, xlo, xhi):
    base = yup.shape[0] - 8
    y = jax.ShapeDtypeStruct(yup.shape, F32)
    return pl.pallas_call(
        functools.partial(corners_kernel, base),
        out_shape=(y, y),
        in_specs=[SMEM, ANY, ANY, VMEM, VMEM],
        out_specs=[ANY, ANY],
        input_output_aliases={1: 0, 2: 1},
        scratch_shapes=[pltpu.VMEM((2, 8, NZ), F32), pltpu.SemaphoreType.DMA((2,))],
        compiler_params=pltpu.CompilerParams(vmem_limit_bytes=LIMIT),
        name="corners",
    )(meta, yup, ydn, xlo, xhi)


def inverse(value):
    guess = pl.reciprocal(value, approx=True)
    guess = guess * (2.0 - value * guess)
    return guess * (2.0 - value * guess)


def lanes_both_ways(here):
    lane = lax.broadcasted_iota(jnp.int32, here.shape, 1)
    before = jnp.where(lane > 0, pltpu.roll(here, 1, 1), 0.0)
    after = jnp.where(lane < NZ - 1, pltpu.roll(here, NZ - 1, 1), 0.0)
    return before + after


def advance(here, beside, before, courant, absorb):
    inv = inverse(1.0 + absorb)
    return before + (2.0 * inv) * (here - before) + (courant * inv) * (beside - 6.0 * here)


CHUNKS = 4
ROWS = CX // CHUNKS
BLOCK = (CX, CY, NZ)
PADDED = (CX + 2, CY + 16, NZ)


def clear_rim(pe):
    edge = jnp.zeros((CX, 8, NZ), F32)
    pe[1 : CX + 1, 0:8, :] = edge
    pe[1 : CX + 1, CY + 8 : CY + 16, :] = edge
    pe[0] = jnp.zeros((CY + 16, NZ), F32)
    pe[CX + 1] = jnp.zeros((CY + 16, NZ), F32)


def around(pe, x):
    here = pe[x + 1, 8 : CY + 8, :]
    beside = pe[x, 8 : CY + 8, :] + pe[x + 2, 8 : CY + 8, :]
    beside = beside + pe[x + 1, 7 : CY + 7, :] + pe[x + 1, 9 : CY + 9, :]
    return here, beside + lanes_both_ways(here)


def first_inner_kernel(p, q, c, a, raw, two, side, here_out, pe, qs, cs, as_, sem):
    copies = []
    for n in range(CHUNKS):
        s = slice(ROWS * n, ROWS * n + ROWS)
        to_rows = slice(1 + ROWS * n, 1 + ROWS * n + ROWS)
        part = [pltpu.make_async_copy(p.at[s], pe.at[to_rows, 8 : CY + 8, :], sem.at[0, n])]
        for m, (ref, to) in enumerate(((q, qs), (c, cs), (a, as_))):
            part.append(pltpu.make_async_copy(ref.at[s], to.at[s], sem.at[m + 1, n]))
        copies.append(part)
    for part in copies:
        for copy in part:
            copy.start()
    clear_rim(pe)
    copies[0][0].wait()

    def body(x, carry):
        here, beside = around(pe, x)
        inv = inverse(1.0 + as_[x])
        twice = 2.0 * inv
        weight = cs[x] * inv
        two[x] = twice
        side[x] = weight
        here_out[x] = here
        raw[x] = qs[x] + twice * (here - qs[x]) + weight * (beside - 6.0 * here)
        return carry

    for n in range(CHUNKS):
        if n + 1 < CHUNKS:
            copies[n + 1][0].wait()
        for copy in copies[n][1:]:
            copy.wait()
        lax.fori_loop(ROWS * n, ROWS * n + ROWS, body, 0, unroll=8)


def first_inner(p, q, c, a):
    block = jax.ShapeDtypeStruct(BLOCK, F32)
    return pl.pallas_call(
        first_inner_kernel,
        out_shape=(block, block, block, block),
        in_specs=[HBM] * 4,
        out_specs=[VMEM] * 4,
        scratch_shapes=[
            pltpu.VMEM(PADDED, F32),
            pltpu.VMEM(BLOCK, F32),
            pltpu.VMEM(BLOCK, F32),
            pltpu.VMEM(BLOCK, F32),
            pltpu.SemaphoreType.DMA((4, CHUNKS)),
        ],
        compiler_params=pltpu.CompilerParams(vmem_limit_bytes=LIMIT),
        cost_estimate=pl.CostEstimate(flops=12000000, bytes_accessed=10000000, transcendentals=0),
        name="first_inner",
    )(*[far(v) for v in (p, q, c, a)])


def second_inner_kernel(p, q, two, side, raw, out, pe, sem):
    store = pltpu.make_async_copy(p, out, sem)
    store.start()
    clear_rim(pe)

    def fill(x, carry):
        pe[x + 1, 8 : CY + 8, :] = p[x]
        return carry

    lax.fori_loop(0, CX, fill, 0, unroll=8)

    def body(x, carry):
        here, beside = around(pe, x)
        raw[x] = q[x] + two[x] * (here - q[x]) + side[x] * (beside - 6.0 * here)
        return carry

    lax.fori_loop(0, CX, body, 0, unroll=8)
    store.wait()


def second_inner(p, q, two, side):
    return pl.pallas_call(
        second_inner_kernel,
        out_shape=(jax.ShapeDtypeStruct(BLOCK, F32),) * 2,
        in_specs=[VMEM] * 4,
        out_specs=[VMEM, ANY],
        scratch_shapes=[pltpu.VMEM(PADDED, F32), pltpu.SemaphoreType.DMA],
        compiler_params=pltpu.CompilerParams(vmem_limit_bytes=LIMIT),
        cost_estimate=pl.CostEstimate(flops=12000000, bytes_accessed=8000000, transcendentals=0),
        name="second_inner",
    )(p, q, two, side)


def coarse_kernel(
    first,
    meta,
    p,
    raw,
    weight,
    pxlo,
    pxhi,
    pylo,
    pyhi,
    exlo,
    exhi,
    eylo,
    eyhi,
    new,
    face0,
    face1,
    face2,
    face3,
    rim,
    ring,
    faces,
):
    tile, bulk = meta[22], meta[23]
    inside_grid = (tile > 0, tile < 7, bulk > 0, bulk < 15)
    base = pylo.shape[0] - 8
    qlo, qhi = (2, 2) if first else (1, 0)

    def keep(n, value):
        return jnp.where(inside_grid[n], value, 0.0)

    def body(x, carry):
        new[x] = raw[x]
        return carry

    lax.fori_loop(0, CX, body, 0, unroll=8)

    def plane(ref, y):
        return ref.reshape(CX * CY, NZ)[pl.ds(y, CX, stride=CY), :]

    def corner(n, ref, at):
        return keep(n, ref[base + at : base + at + 1, :])

    def extra(ref, n):
        return ref[n] if len(ref.shape) == 3 else ref[64 * n : 64 * n + 64, :]

    sides = (
        (pxlo[1], pxlo[0], p[0], corner(2, pylo, 0), corner(3, pyhi, 0), exlo, qlo),
        (pxhi[0], pxhi[1], p[CX - 1], corner(2, pylo, 1), corner(3, pyhi, 1), exhi, qhi),
        (pylo[64:128, :], pylo[0:64, :], plane(p, 0), *[pylo[base + n : base + n + 1, :] for n in (0, 1)], eylo, qlo),
        (pyhi[0:64, :], pyhi[64:128, :], plane(p, CY - 1), *[pyhi[base + n : base + n + 1, :] for n in (0, 1)], eyhi, qhi),
    )
    for n, (here, out, inside, before, after, ref, at_q) in enumerate(sides):
        here = keep(n, here)
        rim[0, n] = here
        ring[n, 7:8, :] = keep(n, before)
        ring[n, 8:72, :] = here
        ring[n, 72:73, :] = keep(n, after)
        beside = ring[n, 7:71, :] + ring[n, 9:73, :] + keep(n, out) + inside + lanes_both_ways(here)
        rim[1, n] = advance(here, beside, *[keep(n, extra(ref, m)) for m in (at_q, 3, 4)])

    new[0] = new[0] + weight[0] * rim[0, 0]
    new[CX - 1] = new[CX - 1] + weight[CX - 1] * rim[0, 1]
    low = (plane(weight, 0) * rim[0, 2])[:, None, :]
    new[:, 0:1, :] = new[:, 0:1, :] + low
    high = (plane(weight, CY - 1) * rim[0, 3])[:, None, :]
    new[:, CY - 1 : CY, :] = new[:, CY - 1 : CY, :] + high

    from_z = lax.broadcasted_iota(jnp.int32, (NZ, NZ), 0)
    to_lane = lax.broadcasted_iota(jnp.int32, (NZ, NZ), 1)
    out_lane = lax.broadcasted_iota(jnp.int32, (BC, NZ), 1)
    deep_lane = lax.broadcasted_iota(jnp.int32, (BC, BC, NZ), 2)
    deep_y = lax.broadcasted_iota(jnp.int32, (BC, BC, NZ), 1)
    diagonal = (deep_lane & 15) == deep_y

    def entry(k, carry):
        ident = meta[k]

        @pl.when(ident >= 0)
        def _():
            ox = pl.multiple_of(meta[4 + k], 16)
            oy = pl.multiple_of(meta[8 + k], 16)
            oz = meta[12 + k]
            where_to = partner_of(meta, ident >> 1) * 2 + (ident & 1)
            low_face = (to_lane >= 32) & (to_lane < 48)
            high_face = (to_lane >= 48) & (to_lane < 64)
            source = jnp.where(
                low_face, oz - 1, jnp.where(high_face, oz + BC, oz + (to_lane & 15))
            )
            mover = jnp.where(from_z == source, 1.0, 0.0).astype(BF16)
            mover = jnp.concatenate([mover, mover], axis=0)
            for t, ref in enumerate((p, new)):
                cube = ref[pl.ds(ox, BC), pl.ds(oy, BC), :].reshape(BC * BC, NZ)
                y = pl.multiple_of(jnp.maximum(oy - 8, 0), 8)
                ym = ref[pl.ds(ox, BC), pl.ds(y, 8), :][:, 7, :]
                ym = jnp.where(oy == 0, rim[t, 2, pl.ds(ox, BC), :], ym)
                y = pl.multiple_of(jnp.minimum(oy + BC, CY - 8), 8)
                yp = ref[pl.ds(ox, BC), pl.ds(y, 8), :][:, 0, :]
                yp = jnp.where(oy == CY - BC, rim[t, 3, pl.ds(ox, BC), :], yp)
                xm = ref[jnp.maximum(ox - 1, 0), pl.ds(oy, BC), :]
                xm = jnp.where(ox == 0, rim[t, 0, pl.ds(oy, BC), :], xm)
                xp = ref[jnp.minimum(ox + BC, CX - 1), pl.ds(oy, BC), :]
                xp = jnp.where(ox == CX - BC, rim[t, 1, pl.ds(oy, BC), :], xp)
                high, low = split(jnp.concatenate([cube, ym, yp, xm, xp], axis=0))
                moved = dot(jnp.concatenate([high, low], axis=1), mover)
                z_face = jnp.where(diagonal, moved[0:256].reshape(BC, BC, NZ), 0.0).sum(axis=1)
                tile_ = jnp.where(out_lane < 80, moved[288:304], moved[304:320])
                tile_ = jnp.where(out_lane < 64, z_face, tile_)
                tile_ = jnp.where(out_lane < 32, moved[272:288], tile_)
                tile_ = jnp.where(out_lane < 16, moved[256:272], tile_)
                faces[where_to, t] = tile_

        return carry

    lax.fori_loop(0, MOST, entry, 0)
    for n, ref in enumerate((face0, face1, face2, face3)):
        ref[...] = faces[2 * n : 2 * n + 2]


def coarse(first, meta, p, raw, weight, halos, extras):
    face = jax.ShapeDtypeStruct((2, 2, BC, NZ), F32)
    return pl.pallas_call(
        functools.partial(coarse_kernel, first),
        out_shape=(jax.ShapeDtypeStruct(BLOCK, F32), face, face, face, face),
        in_specs=[SMEM] + [VMEM] * 11,
        out_specs=[VMEM] * 5,
        scratch_shapes=[
            pltpu.VMEM((2, 4, 64, NZ), F32),
            pltpu.VMEM((4, 80, NZ), F32),
            pltpu.VMEM((8, 2, BC, NZ), F32),
        ],
        compiler_params=pltpu.CompilerParams(vmem_limit_bytes=LIMIT),
        name="coarse",
    )(meta, p, raw, weight, *halos, *extras)


def factors_kernel(c, a, one, two, three, cs, as_, sem):
    copies = []
    for j in range(2):
        copies.append(pltpu.make_async_copy(c.at[j], cs.at[j], sem.at[2 * j]))
        copies.append(pltpu.make_async_copy(a.at[j], as_.at[j], sem.at[2 * j + 1]))
    for copy in copies:
        copy.start()
    for j in range(2):
        copies[2 * j].wait()
        copies[2 * j + 1].wait()

        def body(i, carry):
            s = pl.ds(pl.multiple_of(8 * i, 8), 8)
            inv = inverse(1.0 + as_[j, s, :])
            side = cs[j, s, :] * inv
            three[j, s, :] = side
            one[j, s, :] = 2.0 * inv - 6.0 * side
            two[j, s, :] = 1.0 - 2.0 * inv
            return carry

        lax.fori_loop(0, FINE // 8, body, 0)


def factors(c, a):
    box = jax.ShapeDtypeStruct((2, FINE, PLANE), F32)
    return pl.pallas_call(
        factors_kernel,
        out_shape=(box, box, box),
        in_specs=[HBM] * 2,
        out_specs=[VMEM] * 3,
        scratch_shapes=[pltpu.VMEM(box.shape, F32)] * 2 + [pltpu.SemaphoreType.DMA((4,))],
        compiler_params=pltpu.CompilerParams(vmem_limit_bytes=LIMIT),
        cost_estimate=pl.CostEstimate(flops=3000000, bytes_accessed=4000000, transcendentals=0),
        name="factors",
    )(far(c), far(a))


def turned(v):
    return {d: (pltpu.roll(v, d, 1), pltpu.roll(v, 128 - d, 1)) for d in (1, 48)}


def beside_in_plane(row, masks):
    small = lax.broadcasted_iota(jnp.int32, (8, 128), 1)
    zero = jnp.zeros((8, 128), F32)
    none = {d: (zero, zero) for d in (1, 48)}
    cur = row(0)
    cur_t = turned(cur)
    before_t = none
    for k in range(PLANE // 128):
        ls = slice(128 * k, 128 * k + 128)
        last = k + 1 == PLANE // 128
        nxt = cur if last else row(k + 1)
        nxt_t = none if last else turned(nxt)
        total = jnp.where(small < 48, before_t[48][0], cur_t[48][0])
        total = total + jnp.where(small >= 80, nxt_t[48][1], cur_t[48][1])
        down = jnp.where(small < 1, before_t[1][0], cur_t[1][0])
        up = jnp.where(small >= 127, nxt_t[1][1], cur_t[1][1])
        total = total + down * masks[0, :, ls] + up * masks[1, :, ls]
        yield ls, cur, total
        before_t, cur, cur_t = cur_t, nxt, nxt_t


def ahead_kernel(f, g, one, two, three, masks, raw, buf, sem):
    copies = [pltpu.make_async_copy(f.at[j], buf.at[j, 8:56, :], sem.at[j]) for j in range(2)]
    for copy in copies:
        copy.start()
    for j in range(2):
        buf[j, 0:8, :] = jnp.zeros((8, PLANE), F32)
        buf[j, 56:64, :] = jnp.zeros((8, PLANE), F32)
    for copy in copies:
        copy.wait()

    def box(j, carry):
        for i in range(6):
            s = slice(8 * i, 8 * i + 8)

            def row(k):
                return buf[j, 8 + 8 * i : 16 + 8 * i, 128 * k : 128 * k + 128]

            for ls, cur, total in beside_in_plane(row, masks):
                total = total + buf[j, 7 + 8 * i : 15 + 8 * i, ls] + buf[j, 9 + 8 * i : 17 + 8 * i, ls]
                raw[j, s, ls] = (
                    one[j, s, ls] * cur + two[j, s, ls] * g[j, s, ls] + three[j, s, ls] * total
                )
        return carry

    lax.fori_loop(0, 2, box, 0)


def ahead(f, g, weights, masks):
    box = jax.ShapeDtypeStruct((2, FINE, PLANE), F32)
    return pl.pallas_call(
        ahead_kernel,
        out_shape=box,
        in_specs=[ANY] + [VMEM] * 5,
        out_specs=VMEM,
        scratch_shapes=[pltpu.VMEM((2, 64, PLANE), F32), pltpu.SemaphoreType.DMA((2,))],
        compiler_params=pltpu.CompilerParams(vmem_limit_bytes=LIMIT),
        cost_estimate=pl.CostEstimate(flops=5000000, bytes_accessed=5000000, transcendentals=0),
        name="ahead",
    )(f, g, *weights, masks)


def fine_kernel(
    meta,
    f,
    raw,
    one,
    two,
    three,
    r0,
    r1,
    r2,
    r3,
    masks,
    spread,
    pick,
    pool,
    f_out,
    g_out,
    res,
    buf,
    ghost,
    xrow,
    faces,
    sem,
):
    copy = pltpu.make_async_copy(f, buf.at[0, :, 8:56, :], sem.at[0])
    copy.start()
    for n, ref in enumerate((r0, r1, r2, r3)):
        faces[2 * n : 2 * n + 2] = ref[...]

    lane = lax.broadcasted_iota(jnp.int32, (BC, NZ), 1)
    wide_lane = jnp.concatenate([lane, lane], axis=1)
    tall = lax.broadcasted_iota(jnp.int32, (FINE, BC), 0)
    wide = lax.broadcasted_iota(jnp.int32, (FINE, BC), 1)
    thrice = jnp.where((tall >= 3 * wide) & (tall < 3 * wide + 3), 1.0, 0.0).astype(BF16)
    sides, rows = [], []
    for j in range(2):
        source = (meta[16 + 3 * j] >> 6) * 16 + (meta[17 + 3 * j] >> 6)
        at = partner_of(meta, source) * 2 + j
        old = jnp.where(lane < 96, faces[at, 0], 0.0)
        new = jnp.where(lane < 96, faces[at, 1], 0.0)
        for m in range(3):
            high, low = split(old + (m / 3.0) * (new - old))
            both = jnp.concatenate([high, low], axis=1)
            zero = jnp.zeros_like(both)
            sides.append(jnp.where(wide_lane < 64, both, zero))
            rows.append(jnp.where((wide_lane >= 64) & (wide_lane < 80), both, zero))
            rows.append(jnp.where(wide_lane >= 80, both, zero))
    tall_sides = dot(thrice, jnp.concatenate(sides, axis=1)).astype(BF16)
    sides = [tall_sides[:, 256 * n : 256 * n + 256] for n in range(6)]
    spreaded = dot(jnp.concatenate(sides + rows, axis=0), spread[...])
    for j in range(2):
        for m in range(3):
            at = 48 * (3 * j + m)
            ghost[m, j] = spreaded[at : at + 48]
        for n in range(6):
            at = 288 + 16 * (6 * j + n)
            part = spreaded[at : at + 16] * pick[...]
            xrow[j, n : n + 1, :] = part.sum(axis=0, keepdims=True)
    copy.wait()

    def first(j):
        for i in range(6):
            s = slice(8 * i, 8 * i + 8)
            buf[1, j, 8 + 8 * i : 16 + 8 * i, :] = raw[j, s, :] + three[j, s, :] * ghost[0, j, s, :]
        for n, x in ((0, 0), (1, FINE - 1)):
            buf[1, j, 8 + x : 9 + x, :] = (
                buf[1, j, 8 + x : 9 + x, :] + three[j, x : x + 1, :] * xrow[j, n : n + 1, :]
            )

    def substep(m, j):
        now, old = m % 2, 1 - m % 2
        buf[now, j, 7:8, :] = xrow[j, 2 * m : 2 * m + 1, :]
        buf[now, j, 56:57, :] = xrow[j, 2 * m + 1 : 2 * m + 2, :]
        for i in range(6):
            s = slice(8 * i, 8 * i + 8)

            def row(k):
                return buf[now, j, 8 + 8 * i : 16 + 8 * i, 128 * k : 128 * k + 128]

            for ls, cur, total in beside_in_plane(row, masks):
                total = total + ghost[m, j, s, ls]
                total = total + (
                    buf[now, j, 7 + 8 * i : 15 + 8 * i, ls] + buf[now, j, 9 + 8 * i : 17 + 8 * i, ls]
                )
                buf[old, j, 8 + 8 * i : 16 + 8 * i, ls] = (
                    one[j, s, ls] * cur
                    + two[j, s, ls] * buf[old, j, 8 + 8 * i : 16 + 8 * i, ls]
                    + three[j, s, ls] * total
                )

    def box(j, carry):
        first(j)
        substep(1, j)
        substep(2, j)
        return carry

    lax.fori_loop(0, 2, box, 0)
    stores = [
        pltpu.make_async_copy(buf.at[1, :, 8:56, :], f_out, sem.at[0]),
        pltpu.make_async_copy(buf.at[0, :, 8:56, :], g_out, sem.at[1]),
    ]
    for copy in stores:
        copy.start()
    tall = lax.broadcasted_iota(jnp.int32, (BC, FINE), 1)
    wide = lax.broadcasted_iota(jnp.int32, (BC, FINE), 0)
    gather = jnp.where((tall >= 3 * wide) & (tall < 3 * wide + 3), 1.0, 0.0).astype(BF16)
    parts = [part for j in range(2) for part in split(buf[1, j, 8:56, :])]
    pooled = dot(jnp.concatenate(parts, axis=0), pool[...])
    parts = []
    for j in range(2):
        parts += split(pooled[96 * j : 96 * j + 48] + pooled[96 * j + 48 : 96 * j + 96])
    means = dot(gather, jnp.concatenate(parts, axis=1))
    for j in range(2):
        at = 512 * j
        res[j] = (means[:, at : at + 256] + means[:, at + 256 : at + 512]) * (1.0 / 27.0)
    for copy in stores:
        copy.wait()


def fine(meta, f, raw, weights, received, consts):
    box = jax.ShapeDtypeStruct((2, FINE, PLANE), F32)
    return pl.pallas_call(
        fine_kernel,
        out_shape=(box, box, jax.ShapeDtypeStruct((2, BC, BC * BC), F32)),
        in_specs=[SMEM, ANY] + [VMEM] * 12,
        out_specs=[ANY, ANY, VMEM],
        scratch_shapes=[
            pltpu.VMEM((2, 2, 64, PLANE), F32),
            pltpu.VMEM((3, 2, FINE, PLANE), F32),
            pltpu.VMEM((2, 8, PLANE), F32),
            pltpu.VMEM((8, 2, BC, NZ), F32),
            pltpu.SemaphoreType.DMA((2,)),
        ],
        compiler_params=pltpu.CompilerParams(vmem_limit_bytes=LIMIT),
        name="fine",
    )(meta, f, raw, *weights, *received, *consts)


def moved_box(meta, got, k, mine, from_yz, to_lane):
    ident = meta[k]
    value = got[partner_of(meta, ident >> 1) * 2 + (ident & 1)]
    full = jnp.where(mine, value[:, None, :], 0.0).reshape(BC * BC, BC * BC)
    high, low = split(full)
    mover = jnp.where(to_lane == meta[12 + k] + (from_yz & 15), 1.0, 0.0).astype(BF16)
    moved = dot(jnp.concatenate([high, low], axis=1), jnp.concatenate([mover, mover], axis=0))
    return moved.reshape(BC, BC, NZ)


def box_iotas():
    y_of = lax.broadcasted_iota(jnp.int32, (BC, BC, BC * BC), 1)
    lane_of = lax.broadcasted_iota(jnp.int32, (BC, BC, BC * BC), 2)
    from_yz = lax.broadcasted_iota(jnp.int32, (BC * BC, NZ), 0)
    to_lane = lax.broadcasted_iota(jnp.int32, (BC * BC, NZ), 1)
    return (lane_of >> 4) == y_of, from_yz, to_lane


def insert_kernel(meta, new, r0, r1, r2, r3, out, xup, xdn, yup, ydn, got):
    for n, ref in enumerate((r0, r1, r2, r3)):
        got[2 * n : 2 * n + 2] = ref[...]

    def body(x, carry):
        out[x] = new[x]
        return carry

    lax.fori_loop(0, CX, body, 0, unroll=8)
    lane = lax.broadcasted_iota(jnp.int32, (BC, BC, NZ), 2)
    iotas = box_iotas()

    def entry(k, carry):
        @pl.when(meta[k] >= 0)
        def _():
            at = (pl.ds(meta[4 + k], BC), pl.ds(pl.multiple_of(meta[8 + k], 16), BC))
            moved = moved_box(meta, got, k, *iotas)
            oz = meta[12 + k]
            out[at[0], at[1], :] = jnp.where(
                (lane >= oz) & (lane < oz + BC), moved, out[at[0], at[1], :]
            )

        return carry

    lax.fori_loop(0, MOST, entry, 0)

    def plane(y):
        return out.reshape(CX * CY, NZ)[pl.ds(y, CX, stride=CY), :]

    xup[...] = out[CX - 2 : CX]
    xdn[...] = out[0:2]
    yup[0:64, :] = plane(CY - 2)
    yup[64:128, :] = plane(CY - 1)
    ydn[0:64, :] = plane(0)
    ydn[64:128, :] = plane(1)
    yup[128:136, :] = jnp.zeros((8, NZ), F32)
    ydn[128:136, :] = jnp.zeros((8, NZ), F32)


def insert(meta, new, received):
    x = jax.ShapeDtypeStruct((2, CY, NZ), F32)
    y = jax.ShapeDtypeStruct((2 * CX + 8, NZ), F32)
    return pl.pallas_call(
        insert_kernel,
        out_shape=(jax.ShapeDtypeStruct(BLOCK, F32), x, x, y, y),
        in_specs=[SMEM] + [VMEM] * 5,
        out_specs=[VMEM] * 5,
        scratch_shapes=[pltpu.VMEM((8, BC, BC * BC), F32)],
        compiler_params=pltpu.CompilerParams(vmem_limit_bytes=LIMIT),
        name="insert",
    )(meta, new, *received)


def emit_kernel(new, out, sem):
    copy = pltpu.make_async_copy(new, out, sem)
    copy.start()
    copy.wait()


def emit(new):
    return pl.pallas_call(
        emit_kernel,
        out_shape=jax.ShapeDtypeStruct(BLOCK, F32),
        in_specs=[VMEM],
        out_specs=HBM,
        scratch_shapes=[pltpu.SemaphoreType.DMA],
        compiler_params=pltpu.CompilerParams(vmem_limit_bytes=LIMIT),
        cost_estimate=pl.CostEstimate(flops=0, bytes_accessed=6000000, transcendentals=0),
        name="emit",
    )(new)


def finish_kernel(meta, new, r0, r1, r2, r3, out, got, boxes, sem):
    def region(k):
        return out.at[pl.ds(meta[4 + k], BC), pl.ds(pl.multiple_of(meta[8 + k], 16), BC), :]

    slots = []
    for k in range(MOST):
        slot = k
        for n in reversed(range(k)):
            same = (meta[4 + n] == meta[4 + k]) & (meta[8 + n] == meta[8 + k]) & (meta[n] >= 0)
            slot = jnp.where(same, n, slot)
        slots.append(slot)
    valid = [meta[k] >= 0 for k in range(MOST)]
    leads = [valid[k] & (slots[k] == k) for k in range(MOST)]
    for k in range(MOST):

        @pl.when(leads[k])
        def _():
            pltpu.make_async_copy(region(k), boxes.at[k], sem.at[k]).start()

    for n, ref in enumerate((r0, r1, r2, r3)):
        got[2 * n : 2 * n + 2] = ref[...]
    lane = lax.broadcasted_iota(jnp.int32, (BC, BC, NZ), 2)
    iotas = box_iotas()
    for k in range(MOST):

        @pl.when(leads[k])
        def _():
            pltpu.make_async_copy(region(k), boxes.at[k], sem.at[k]).wait()

        @pl.when(valid[k])
        def _():
            moved = moved_box(meta, got, k, *iotas)
            oz = meta[12 + k]
            boxes[slots[k]] = jnp.where((lane >= oz) & (lane < oz + BC), moved, boxes[slots[k]])

    for k in range(MOST):

        @pl.when(leads[k])
        def _():
            pltpu.make_async_copy(boxes.at[k], region(k), sem.at[k]).start()

    for k in range(MOST):

        @pl.when(leads[k])
        def _():
            pltpu.make_async_copy(boxes.at[k], region(k), sem.at[k]).wait()


def finish(meta, new, received):
    return pl.pallas_call(
        finish_kernel,
        out_shape=jax.ShapeDtypeStruct(BLOCK, F32),
        in_specs=[SMEM, ANY] + [VMEM] * 4,
        out_specs=ANY,
        input_output_aliases={1: 0},
        scratch_shapes=[
            pltpu.VMEM((8, BC, BC * BC), F32),
            pltpu.VMEM((MOST, BC, BC, NZ), F32),
            pltpu.SemaphoreType.DMA((MOST,)),
        ],
        compiler_params=pltpu.CompilerParams(vmem_limit_bytes=LIMIT),
        name="finish",
    )(meta, new, *received)


def ring(size, by):
    return [(i, (i + by) % size) for i in range(size)]


def halo(meta, xup, xdn, yup, ydn):
    xlo = lax.ppermute(xup, "tile", ring(8, 1))
    xhi = lax.ppermute(xdn, "tile", ring(8, -1))
    yup, ydn = corners(meta, yup, ydn, xlo, xhi)
    ylo = lax.ppermute(yup, "bulk", ring(16, 1))
    yhi = lax.ppermute(ydn, "bulk", ring(16, -1))
    return xlo, xhi, ylo, yhi


def trade(values):
    done = [values[0]]
    for value, away in zip(values[1:], (1, 64, 65)):
        done.append(lax.ppermute(value, ("tile", "bulk"), [(d, d ^ away) for d in range(128)]))
    return done


def on_device(
    coarse_now,
    coarse_before,
    coarse_courant,
    coarse_absorb,
    fine_now,
    fine_before,
    fine_courant,
    fine_absorb,
    box_anchor,
    intersection,
):
    place = jnp.stack([lax.axis_index("tile"), lax.axis_index("bulk")]).astype(jnp.int32)
    meta = jnp.concatenate([intersection.reshape(16), box_anchor.reshape(6), place])
    consts = tables()
    extras = halo(meta, *edges(coarse_now, coarse_before, coarse_courant, coarse_absorb))
    weights = factors(fine_courant, fine_absorb)
    first = ahead(fine_now, fine_before, weights, consts[0])
    raw, two, side, start = first_inner(coarse_now, coarse_before, coarse_courant, coarse_absorb)
    new, *faces = coarse(True, meta, start, raw, side, extras, extras)
    f, g, res = fine(meta, fine_now, first, weights, trade(faces), consts)
    middle, *packed = insert(meta, new, trade([res] * 4))
    first = ahead(f, g, weights, consts[0])
    halos = halo(meta, *packed)
    raw, q = second_inner(middle, start, two, side)
    new, *faces = coarse(False, meta, middle, raw, side, halos, extras)
    f, g, res = fine(meta, f, first, weights, trade(faces), consts)
    p = finish(meta, emit(new), trade([res] * 4))
    return p, q, f, g


def solution(mesh):
    grid = P("tile", "bulk", None)
    boxes = P(("tile", "bulk"), None, None)
    in_specs = (grid,) * 4 + (boxes,) * 4 + (P(("tile", "bulk"), None), boxes)
    return jax.shard_map(
        on_device, mesh=mesh, in_specs=in_specs, out_specs=(grid, grid, boxes, boxes), check_vma=False
    )
```

```python
import functools

import jax
import jax.numpy as jnp
import numpy as np
from jax import lax
from jax.experimental import pallas as pl
from jax.experimental.pallas import tpu as pltpu
from jax.sharding import PartitionSpec as P

CX = 64
CY = 64
NZ = 128
BC = 16
FINE = 48
PLANE = FINE * FINE
MOST = 4
F32 = jnp.float32
BF16 = jnp.bfloat16
ANY = pl.BlockSpec(memory_space=pl.ANY)
HBM = pl.BlockSpec(memory_space=pltpu.HBM)
VMEM = pl.BlockSpec(memory_space=pltpu.VMEM)
SMEM = pl.BlockSpec(memory_space=pltpu.SMEM)
LIMIT = 20 * 1024 * 1024


def tables():
    flat = np.arange(PLANE)
    y, z = flat // FINE, flat % FINE
    masks = np.stack([z > 0, z < FINE - 1]).astype(np.float32)
    masks = np.repeat(masks[:, None, :], 8, axis=1)
    r = np.arange(BC)[:, None]
    spread = np.zeros((128, PLANE), np.float32)
    spread[0:16] = (y == 0) & (z // 3 == r)
    spread[16:32] = (y == FINE - 1) & (z // 3 == r)
    spread[32:48] = (z == 0) & (y // 3 == r)
    spread[48:64] = (z == FINE - 1) & (y // 3 == r)
    spread[64:80] = z // 3 == r
    spread[80:96] = z // 3 == r
    spread = np.concatenate([spread, spread], axis=0)
    pick = (y // 3 == r).astype(np.float32)
    pool = ((y // 3 * BC + z // 3)[:, None] == np.arange(BC * BC)[None, :]).astype(np.float32)
    return jnp.asarray(masks), jnp.asarray(spread, BF16), jnp.asarray(pick), jnp.asarray(pool, BF16)


def partner_of(meta, device):
    away = (meta[22] * 16 + meta[23]) ^ device
    return (away & 1) + 2 * ((away >> 6) & 1)


def far(value):
    return pltpu.with_memory_space_constraint(value, pltpu.HBM)


def split(value):
    high = value.astype(BF16)
    low = (value - high.astype(F32)).astype(BF16)
    return high, low


def dot(left, right):
    return jnp.dot(left, right, preferred_element_type=F32)


def x_edges_kernel(p, q, c, a, xup, xdn, sem):
    ends = [(p.at[CX - 2 : CX], xup.at[0:2]), (p.at[0:2], xdn.at[0:2])]
    for n, ref in enumerate((q, c, a)):
        ends.append((ref.at[CX - 1], xup.at[n + 2]))
        ends.append((ref.at[0], xdn.at[n + 2]))
    copies = [pltpu.make_async_copy(*pair, sem.at[n]) for n, pair in enumerate(ends)]
    for copy in copies:
        copy.start()
    for copy in copies:
        copy.wait()


def x_edges(p, q, c, a):
    x = jax.ShapeDtypeStruct((5, CY, NZ), F32)
    return pl.pallas_call(
        x_edges_kernel,
        out_shape=(x, x),
        in_specs=[HBM] * 4,
        out_specs=[VMEM] * 2,
        scratch_shapes=[pltpu.SemaphoreType.DMA((8,))],
        compiler_params=pltpu.CompilerParams(vmem_limit_bytes=LIMIT),
        name="x_edges",
    )(*[far(v) for v in (p, q, c, a)])


def y_edges_kernel(p, q, c, a, yup, ydn, tiles, sem):
    ends = []
    for n, ref in enumerate((p, q, c, a)):
        ends.append((ref.at[:, CY - 8 : CY, :], tiles.at[0, n]))
        ends.append((ref.at[:, 0:8, :], tiles.at[1, n]))
    copies = [pltpu.make_async_copy(*pair, sem.at[n]) for n, pair in enumerate(ends)]
    for copy in copies:
        copy.start()
    for copy in copies:
        copy.wait()

    def plane(side, n, y):
        return tiles.at[side, n].reshape(CX * 8, NZ)[pl.ds(y, CX, stride=8), :]

    yup[0:64, :] = plane(0, 0, 6)
    yup[64:128, :] = plane(0, 0, 7)
    ydn[0:64, :] = plane(1, 0, 0)
    ydn[64:128, :] = plane(1, 0, 1)
    for n in range(1, 4):
        yup[64 * (n + 1) : 64 * (n + 2), :] = plane(0, n, 7)
        ydn[64 * (n + 1) : 64 * (n + 2), :] = plane(1, n, 0)
    yup[320:328, :] = jnp.zeros((8, NZ), F32)
    ydn[320:328, :] = jnp.zeros((8, NZ), F32)


def y_edges(p, q, c, a):
    y = jax.ShapeDtypeStruct((5 * CX + 8, NZ), F32)
    return pl.pallas_call(
        y_edges_kernel,
        out_shape=(y, y),
        in_specs=[HBM] * 4,
        out_specs=[VMEM] * 2,
        scratch_shapes=[pltpu.VMEM((2, 4, CX, 8, NZ), F32), pltpu.SemaphoreType.DMA((8,))],
        compiler_params=pltpu.CompilerParams(vmem_limit_bytes=LIMIT),
        cost_estimate=pl.CostEstimate(flops=0, bytes_accessed=5000000, transcendentals=0),
        name="y_edges",
    )(*[far(v) for v in (p, q, c, a)])


def corners_kernel(base, meta, yup, ydn, xlo, xhi, yup_out, ydn_out, rows, sem):
    lo = meta[22] > 0
    hi = meta[22] < 7
    for n, y in ((0, CY - 1), (1, 0)):
        rows[n, 0:1, :] = jnp.where(lo, xlo[1, y : y + 1, :], 0.0)
        rows[n, 1:2, :] = jnp.where(hi, xhi[0, y : y + 1, :], 0.0)
    copies = [
        pltpu.make_async_copy(rows.at[0], yup_out.at[base : base + 8, :], sem.at[0]),
        pltpu.make_async_copy(rows.at[1], ydn_out.at[base : base + 8, :], sem.at[1]),
    ]
    for copy in copies:
        copy.start()
    for copy in copies:
        copy.wait()


def corners(meta, yup, ydn, xlo, xhi):
    base = yup.shape[0] - 8
    y = jax.ShapeDtypeStruct(yup.shape, F32)
    return pl.pallas_call(
        functools.partial(corners_kernel, base),
        out_shape=(y, y),
        in_specs=[SMEM, ANY, ANY, VMEM, VMEM],
        out_specs=[ANY, ANY],
        input_output_aliases={1: 0, 2: 1},
        scratch_shapes=[pltpu.VMEM((2, 8, NZ), F32), pltpu.SemaphoreType.DMA((2,))],
        compiler_params=pltpu.CompilerParams(vmem_limit_bytes=LIMIT),
        name="corners",
    )(meta, yup, ydn, xlo, xhi)


def inverse(value):
    guess = pl.reciprocal(value, approx=True)
    guess = guess * (2.0 - value * guess)
    return guess * (2.0 - value * guess)


def lanes_both_ways(here):
    lane = lax.broadcasted_iota(jnp.int32, here.shape, 1)
    before = jnp.where(lane > 0, pltpu.roll(here, 1, 1), 0.0)
    after = jnp.where(lane < NZ - 1, pltpu.roll(here, NZ - 1, 1), 0.0)
    return before + after


def advance(here, beside, before, courant, absorb):
    inv = inverse(1.0 + absorb)
    return before + (2.0 * inv) * (here - before) + (courant * inv) * (beside - 6.0 * here)


CHUNKS = 4
ROWS = CX // CHUNKS
BLOCK = (CX, CY, NZ)
PADDED = (CX + 2, CY + 16, NZ)


def clear_rim(pe):
    edge = jnp.zeros((CX, 8, NZ), F32)
    pe[1 : CX + 1, 0:8, :] = edge
    pe[1 : CX + 1, CY + 8 : CY + 16, :] = edge
    pe[0] = jnp.zeros((CY + 16, NZ), F32)
    pe[CX + 1] = jnp.zeros((CY + 16, NZ), F32)


def around(pe, x):
    here = pe[x + 1, 8 : CY + 8, :]
    beside = pe[x, 8 : CY + 8, :] + pe[x + 2, 8 : CY + 8, :]
    beside = beside + pe[x + 1, 7 : CY + 7, :] + pe[x + 1, 9 : CY + 9, :]
    return here, beside + lanes_both_ways(here)


def first_inner_kernel(p, q, c, a, raw, two, side, here_out, pe, qs, cs, as_, sem):
    copies = []
    for n in range(CHUNKS):
        s = slice(ROWS * n, ROWS * n + ROWS)
        to_rows = slice(1 + ROWS * n, 1 + ROWS * n + ROWS)
        part = [pltpu.make_async_copy(p.at[s], pe.at[to_rows, 8 : CY + 8, :], sem.at[0, n])]
        for m, (ref, to) in enumerate(((q, qs), (c, cs), (a, as_))):
            part.append(pltpu.make_async_copy(ref.at[s], to.at[s], sem.at[m + 1, n]))
        copies.append(part)
    for part in copies:
        for copy in part:
            copy.start()
    clear_rim(pe)
    copies[0][0].wait()

    def body(x, carry):
        here, beside = around(pe, x)
        inv = inverse(1.0 + as_[x])
        twice = 2.0 * inv
        weight = cs[x] * inv
        two[x] = twice
        side[x] = weight
        here_out[x] = here
        raw[x] = qs[x] + twice * (here - qs[x]) + weight * (beside - 6.0 * here)
        return carry

    for n in range(CHUNKS):
        if n + 1 < CHUNKS:
            copies[n + 1][0].wait()
        for copy in copies[n][1:]:
            copy.wait()
        lax.fori_loop(ROWS * n, ROWS * n + ROWS, body, 0, unroll=8)


def first_inner(p, q, c, a):
    block = jax.ShapeDtypeStruct(BLOCK, F32)
    return pl.pallas_call(
        first_inner_kernel,
        out_shape=(block, block, block, block),
        in_specs=[HBM] * 4,
        out_specs=[VMEM] * 4,
        scratch_shapes=[
            pltpu.VMEM(PADDED, F32),
            pltpu.VMEM(BLOCK, F32),
            pltpu.VMEM(BLOCK, F32),
            pltpu.VMEM(BLOCK, F32),
            pltpu.SemaphoreType.DMA((4, CHUNKS)),
        ],
        compiler_params=pltpu.CompilerParams(vmem_limit_bytes=LIMIT),
        cost_estimate=pl.CostEstimate(flops=12000000, bytes_accessed=10000000, transcendentals=0),
        name="first_inner",
    )(*[far(v) for v in (p, q, c, a)])


def second_inner_kernel(p, q, two, side, raw, out, pe, sem):
    store = pltpu.make_async_copy(p, out, sem)
    store.start()
    clear_rim(pe)

    def fill(x, carry):
        pe[x + 1, 8 : CY + 8, :] = p[x]
        return carry

    lax.fori_loop(0, CX, fill, 0, unroll=8)

    def body(x, carry):
        here, beside = around(pe, x)
        raw[x] = q[x] + two[x] * (here - q[x]) + side[x] * (beside - 6.0 * here)
        return carry

    lax.fori_loop(0, CX, body, 0, unroll=8)
    store.wait()


def second_inner(p, q, two, side):
    return pl.pallas_call(
        second_inner_kernel,
        out_shape=(jax.ShapeDtypeStruct(BLOCK, F32),) * 2,
        in_specs=[VMEM] * 4,
        out_specs=[VMEM, ANY],
        scratch_shapes=[pltpu.VMEM(PADDED, F32), pltpu.SemaphoreType.DMA],
        compiler_params=pltpu.CompilerParams(vmem_limit_bytes=LIMIT),
        cost_estimate=pl.CostEstimate(flops=12000000, bytes_accessed=8000000, transcendentals=0),
        name="second_inner",
    )(p, q, two, side)


def coarse_kernel(
    first,
    meta,
    p,
    raw,
    weight,
    pxlo,
    pxhi,
    pylo,
    pyhi,
    exlo,
    exhi,
    eylo,
    eyhi,
    new,
    face0,
    face1,
    face2,
    face3,
    rim,
    ring,
    faces,
):
    tile, bulk = meta[22], meta[23]
    inside_grid = (tile > 0, tile < 7, bulk > 0, bulk < 15)
    base = pylo.shape[0] - 8
    qlo, qhi = (2, 2) if first else (1, 0)

    def keep(n, value):
        return jnp.where(inside_grid[n], value, 0.0)

    def body(x, carry):
        new[x] = raw[x]
        return carry

    lax.fori_loop(0, CX, body, 0, unroll=8)

    def plane(ref, y):
        return ref.reshape(CX * CY, NZ)[pl.ds(y, CX, stride=CY), :]

    def corner(n, ref, at):
        return keep(n, ref[base + at : base + at + 1, :])

    def extra(ref, n):
        return ref[n] if len(ref.shape) == 3 else ref[64 * n : 64 * n + 64, :]

    sides = (
        (pxlo[1], pxlo[0], p[0], corner(2, pylo, 0), corner(3, pyhi, 0), exlo, qlo),
        (pxhi[0], pxhi[1], p[CX - 1], corner(2, pylo, 1), corner(3, pyhi, 1), exhi, qhi),
        (pylo[64:128, :], pylo[0:64, :], plane(p, 0), *[pylo[base + n : base + n + 1, :] for n in (0, 1)], eylo, qlo),
        (pyhi[0:64, :], pyhi[64:128, :], plane(p, CY - 1), *[pyhi[base + n : base + n + 1, :] for n in (0, 1)], eyhi, qhi),
    )
    for n, (here, out, inside, before, after, ref, at_q) in enumerate(sides):
        here = keep(n, here)
        rim[0, n] = here
        ring[n, 7:8, :] = keep(n, before)
        ring[n, 8:72, :] = here
        ring[n, 72:73, :] = keep(n, after)
        beside = ring[n, 7:71, :] + ring[n, 9:73, :] + keep(n, out) + inside + lanes_both_ways(here)
        rim[1, n] = advance(here, beside, *[keep(n, extra(ref, m)) for m in (at_q, 3, 4)])

    new[0] = new[0] + weight[0] * rim[0, 0]
    new[CX - 1] = new[CX - 1] + weight[CX - 1] * rim[0, 1]
    low = (plane(weight, 0) * rim[0, 2])[:, None, :]
    new[:, 0:1, :] = new[:, 0:1, :] + low
    high = (plane(weight, CY - 1) * rim[0, 3])[:, None, :]
    new[:, CY - 1 : CY, :] = new[:, CY - 1 : CY, :] + high

    from_z = lax.broadcasted_iota(jnp.int32, (NZ, NZ), 0)
    to_lane = lax.broadcasted_iota(jnp.int32, (NZ, NZ), 1)
    out_lane = lax.broadcasted_iota(jnp.int32, (BC, NZ), 1)
    deep_lane = lax.broadcasted_iota(jnp.int32, (BC, BC, NZ), 2)
    deep_y = lax.broadcasted_iota(jnp.int32, (BC, BC, NZ), 1)
    diagonal = (deep_lane & 15) == deep_y

    def entry(k, carry):
        ident = meta[k]

        @pl.when(ident >= 0)
        def _():
            ox = pl.multiple_of(meta[4 + k], 16)
            oy = pl.multiple_of(meta[8 + k], 16)
            oz = meta[12 + k]
            where_to = partner_of(meta, ident >> 1) * 2 + (ident & 1)
            low_face = (to_lane >= 32) & (to_lane < 48)
            high_face = (to_lane >= 48) & (to_lane < 64)
            source = jnp.where(
                low_face, oz - 1, jnp.where(high_face, oz + BC, oz + (to_lane & 15))
            )
            mover = jnp.where(from_z == source, 1.0, 0.0).astype(BF16)
            mover = jnp.concatenate([mover, mover], axis=0)
            for t, ref in enumerate((p, new)):
                cube = ref[pl.ds(ox, BC), pl.ds(oy, BC), :].reshape(BC * BC, NZ)
                y = pl.multiple_of(jnp.maximum(oy - 8, 0), 8)
                ym = ref[pl.ds(ox, BC), pl.ds(y, 8), :][:, 7, :]
                ym = jnp.where(oy == 0, rim[t, 2, pl.ds(ox, BC), :], ym)
                y = pl.multiple_of(jnp.minimum(oy + BC, CY - 8), 8)
                yp = ref[pl.ds(ox, BC), pl.ds(y, 8), :][:, 0, :]
                yp = jnp.where(oy == CY - BC, rim[t, 3, pl.ds(ox, BC), :], yp)
                xm = ref[jnp.maximum(ox - 1, 0), pl.ds(oy, BC), :]
                xm = jnp.where(ox == 0, rim[t, 0, pl.ds(oy, BC), :], xm)
                xp = ref[jnp.minimum(ox + BC, CX - 1), pl.ds(oy, BC), :]
                xp = jnp.where(ox == CX - BC, rim[t, 1, pl.ds(oy, BC), :], xp)
                high, low = split(jnp.concatenate([cube, ym, yp, xm, xp], axis=0))
                moved = dot(jnp.concatenate([high, low], axis=1), mover)
                z_face = jnp.where(diagonal, moved[0:256].reshape(BC, BC, NZ), 0.0).sum(axis=1)
                tile_ = jnp.where(out_lane < 80, moved[288:304], moved[304:320])
                tile_ = jnp.where(out_lane < 64, z_face, tile_)
                tile_ = jnp.where(out_lane < 32, moved[272:288], tile_)
                tile_ = jnp.where(out_lane < 16, moved[256:272], tile_)
                faces[where_to, t] = tile_

        return carry

    lax.fori_loop(0, MOST, entry, 0)
    for n, ref in enumerate((face0, face1, face2, face3)):
        ref[...] = faces[2 * n : 2 * n + 2]


def coarse(first, meta, p, raw, weight, halos, extras):
    face = jax.ShapeDtypeStruct((2, 2, BC, NZ), F32)
    return pl.pallas_call(
        functools.partial(coarse_kernel, first),
        out_shape=(jax.ShapeDtypeStruct(BLOCK, F32), face, face, face, face),
        in_specs=[SMEM] + [VMEM] * 11,
        out_specs=[VMEM] * 5,
        scratch_shapes=[
            pltpu.VMEM((2, 4, 64, NZ), F32),
            pltpu.VMEM((4, 80, NZ), F32),
            pltpu.VMEM((8, 2, BC, NZ), F32),
        ],
        compiler_params=pltpu.CompilerParams(vmem_limit_bytes=LIMIT),
        name="coarse",
    )(meta, p, raw, weight, *halos, *extras)


def factors_kernel(c, a, one, two, three, cs, as_, sem):
    copies = []
    for j in range(2):
        copies.append(pltpu.make_async_copy(c.at[j], cs.at[j], sem.at[2 * j]))
        copies.append(pltpu.make_async_copy(a.at[j], as_.at[j], sem.at[2 * j + 1]))
    for copy in copies:
        copy.start()
    for j in range(2):
        copies[2 * j].wait()
        copies[2 * j + 1].wait()

        def body(i, carry):
            s = pl.ds(pl.multiple_of(8 * i, 8), 8)
            inv = inverse(1.0 + as_[j, s, :])
            side = cs[j, s, :] * inv
            three[j, s, :] = side
            one[j, s, :] = 2.0 * inv - 6.0 * side
            two[j, s, :] = 1.0 - 2.0 * inv
            return carry

        lax.fori_loop(0, FINE // 8, body, 0)


def factors(c, a):
    box = jax.ShapeDtypeStruct((2, FINE, PLANE), F32)
    return pl.pallas_call(
        factors_kernel,
        out_shape=(box, box, box),
        in_specs=[HBM] * 2,
        out_specs=[VMEM] * 3,
        scratch_shapes=[pltpu.VMEM(box.shape, F32)] * 2 + [pltpu.SemaphoreType.DMA((4,))],
        compiler_params=pltpu.CompilerParams(vmem_limit_bytes=LIMIT),
        cost_estimate=pl.CostEstimate(flops=3000000, bytes_accessed=4000000, transcendentals=0),
        name="factors",
    )(far(c), far(a))


def turned(v):
    return {d: (pltpu.roll(v, d, 1), pltpu.roll(v, 128 - d, 1)) for d in (1, 48)}


def beside_in_plane(row, masks):
    small = lax.broadcasted_iota(jnp.int32, (8, 128), 1)
    zero = jnp.zeros((8, 128), F32)
    none = {d: (zero, zero) for d in (1, 48)}
    cur = row(0)
    cur_t = turned(cur)
    before_t = none
    for k in range(PLANE // 128):
        ls = slice(128 * k, 128 * k + 128)
        last = k + 1 == PLANE // 128
        nxt = cur if last else row(k + 1)
        nxt_t = none if last else turned(nxt)
        total = jnp.where(small < 48, before_t[48][0], cur_t[48][0])
        total = total + jnp.where(small >= 80, nxt_t[48][1], cur_t[48][1])
        down = jnp.where(small < 1, before_t[1][0], cur_t[1][0])
        up = jnp.where(small >= 127, nxt_t[1][1], cur_t[1][1])
        total = total + down * masks[0, :, ls] + up * masks[1, :, ls]
        yield ls, cur, total
        before_t, cur, cur_t = cur_t, nxt, nxt_t


def ahead_kernel(f, g, one, two, three, masks, raw, buf, sem):
    copies = [pltpu.make_async_copy(f.at[j], buf.at[j, 8:56, :], sem.at[j]) for j in range(2)]
    for copy in copies:
        copy.start()
    for j in range(2):
        buf[j, 0:8, :] = jnp.zeros((8, PLANE), F32)
        buf[j, 56:64, :] = jnp.zeros((8, PLANE), F32)
    for copy in copies:
        copy.wait()

    def box(j, carry):
        for i in range(6):
            s = slice(8 * i, 8 * i + 8)

            def row(k):
                return buf[j, 8 + 8 * i : 16 + 8 * i, 128 * k : 128 * k + 128]

            for ls, cur, total in beside_in_plane(row, masks):
                total = total + buf[j, 7 + 8 * i : 15 + 8 * i, ls] + buf[j, 9 + 8 * i : 17 + 8 * i, ls]
                raw[j, s, ls] = (
                    one[j, s, ls] * cur + two[j, s, ls] * g[j, s, ls] + three[j, s, ls] * total
                )
        return carry

    lax.fori_loop(0, 2, box, 0)


def ahead(f, g, weights, masks):
    box = jax.ShapeDtypeStruct((2, FINE, PLANE), F32)
    return pl.pallas_call(
        ahead_kernel,
        out_shape=box,
        in_specs=[ANY] + [VMEM] * 5,
        out_specs=VMEM,
        scratch_shapes=[pltpu.VMEM((2, 64, PLANE), F32), pltpu.SemaphoreType.DMA((2,))],
        compiler_params=pltpu.CompilerParams(vmem_limit_bytes=LIMIT),
        cost_estimate=pl.CostEstimate(flops=5000000, bytes_accessed=5000000, transcendentals=0),
        name="ahead",
    )(f, g, *weights, masks)


def fine_kernel(
    meta,
    f,
    raw,
    one,
    two,
    three,
    r0,
    r1,
    r2,
    r3,
    masks,
    spread,
    pick,
    pool,
    f_out,
    g_out,
    res,
    buf,
    ghost,
    xrow,
    faces,
):
    for n, ref in enumerate((r0, r1, r2, r3)):
        faces[2 * n : 2 * n + 2] = ref[...]

    lane = lax.broadcasted_iota(jnp.int32, (BC, NZ), 1)
    wide_lane = jnp.concatenate([lane, lane], axis=1)
    tall = lax.broadcasted_iota(jnp.int32, (FINE, BC), 0)
    wide = lax.broadcasted_iota(jnp.int32, (FINE, BC), 1)
    thrice = jnp.where((tall >= 3 * wide) & (tall < 3 * wide + 3), 1.0, 0.0).astype(BF16)
    sides, rows = [], []
    for j in range(2):
        source = (meta[16 + 3 * j] >> 6) * 16 + (meta[17 + 3 * j] >> 6)
        at = partner_of(meta, source) * 2 + j
        old = jnp.where(lane < 96, faces[at, 0], 0.0)
        new = jnp.where(lane < 96, faces[at, 1], 0.0)
        for m in range(3):
            high, low = split(old + (m / 3.0) * (new - old))
            both = jnp.concatenate([high, low], axis=1)
            zero = jnp.zeros_like(both)
            sides.append(jnp.where(wide_lane < 64, both, zero))
            rows.append(jnp.where((wide_lane >= 64) & (wide_lane < 80), both, zero))
            rows.append(jnp.where(wide_lane >= 80, both, zero))
    tall_sides = dot(thrice, jnp.concatenate(sides, axis=1)).astype(BF16)
    sides = [tall_sides[:, 256 * n : 256 * n + 256] for n in range(6)]
    spreaded = dot(jnp.concatenate(sides + rows, axis=0), spread[...])
    for j in range(2):
        for m in range(3):
            at = 48 * (3 * j + m)
            ghost[m, j] = spreaded[at : at + 48]
        for n in range(6):
            at = 288 + 16 * (6 * j + n)
            part = spreaded[at : at + 16] * pick[...]
            xrow[j, n : n + 1, :] = part.sum(axis=0, keepdims=True)

    def first(j):
        for i in range(6):
            s = slice(8 * i, 8 * i + 8)
            buf[0, j, 8 + 8 * i : 16 + 8 * i, :] = raw[j, s, :] + three[j, s, :] * ghost[0, j, s, :]
        for n, x in ((0, 0), (1, FINE - 1)):
            buf[0, j, 8 + x : 9 + x, :] = (
                buf[0, j, 8 + x : 9 + x, :] + three[j, x : x + 1, :] * xrow[j, n : n + 1, :]
            )

    def substep(m, j):
        buf[m - 1, j, 7:8, :] = xrow[j, 2 * m : 2 * m + 1, :]
        buf[m - 1, j, 56:57, :] = xrow[j, 2 * m + 1 : 2 * m + 2, :]
        for i in range(6):
            s = slice(8 * i, 8 * i + 8)
            pad = slice(8 + 8 * i, 16 + 8 * i)

            def row(k):
                return buf[m - 1, j, pad, 128 * k : 128 * k + 128]

            for ls, cur, total in beside_in_plane(row, masks):
                total = total + ghost[m, j, s, ls]
                total = total + (
                    buf[m - 1, j, 7 + 8 * i : 15 + 8 * i, ls]
                    + buf[m - 1, j, 9 + 8 * i : 17 + 8 * i, ls]
                )
                old = f[j, s, ls] if m == 1 else buf[0, j, pad, ls]
                value = one[j, s, ls] * cur + two[j, s, ls] * old + three[j, s, ls] * total
                if m == 1:
                    buf[1, j, pad, ls] = value
                    g_out[j, s, ls] = value
                else:
                    f_out[j, s, ls] = value

    def box(j, carry):
        first(j)
        substep(1, j)
        substep(2, j)
        return carry

    lax.fori_loop(0, 2, box, 0)
    tall = lax.broadcasted_iota(jnp.int32, (BC, FINE), 1)
    wide = lax.broadcasted_iota(jnp.int32, (BC, FINE), 0)
    gather = jnp.where((tall >= 3 * wide) & (tall < 3 * wide + 3), 1.0, 0.0).astype(BF16)
    parts = [part for j in range(2) for part in split(f_out[j])]
    pooled = dot(jnp.concatenate(parts, axis=0), pool[...])
    parts = []
    for j in range(2):
        parts += split(pooled[96 * j : 96 * j + 48] + pooled[96 * j + 48 : 96 * j + 96])
    means = dot(gather, jnp.concatenate(parts, axis=1))
    for j in range(2):
        at = 512 * j
        res[j] = (means[:, at : at + 256] + means[:, at + 256 : at + 512]) * (1.0 / 27.0)


def fine(meta, f, raw, weights, received, consts):
    box = jax.ShapeDtypeStruct((2, FINE, PLANE), F32)
    return pl.pallas_call(
        fine_kernel,
        out_shape=(box, box, jax.ShapeDtypeStruct((2, BC, BC * BC), F32)),
        in_specs=[SMEM] + [VMEM] * 13,
        out_specs=[VMEM] * 3,
        scratch_shapes=[
            pltpu.VMEM((2, 2, 64, PLANE), F32),
            pltpu.VMEM((3, 2, FINE, PLANE), F32),
            pltpu.VMEM((2, 8, PLANE), F32),
            pltpu.VMEM((8, 2, BC, NZ), F32),
        ],
        compiler_params=pltpu.CompilerParams(vmem_limit_bytes=LIMIT),
        name="fine",
    )(meta, f, raw, *weights, *received, *consts)


def moved_box(meta, got, k, mine, from_yz, to_lane):
    ident = meta[k]
    value = got[partner_of(meta, ident >> 1) * 2 + (ident & 1)]
    full = jnp.where(mine, value[:, None, :], 0.0).reshape(BC * BC, BC * BC)
    high, low = split(full)
    mover = jnp.where(to_lane == meta[12 + k] + (from_yz & 15), 1.0, 0.0).astype(BF16)
    moved = dot(jnp.concatenate([high, low], axis=1), jnp.concatenate([mover, mover], axis=0))
    return moved.reshape(BC, BC, NZ)


def box_iotas():
    y_of = lax.broadcasted_iota(jnp.int32, (BC, BC, BC * BC), 1)
    lane_of = lax.broadcasted_iota(jnp.int32, (BC, BC, BC * BC), 2)
    from_yz = lax.broadcasted_iota(jnp.int32, (BC * BC, NZ), 0)
    to_lane = lax.broadcasted_iota(jnp.int32, (BC * BC, NZ), 1)
    return (lane_of >> 4) == y_of, from_yz, to_lane


def insert_kernel(meta, new, r0, r1, r2, r3, out, xup, xdn, yup, ydn, got):
    for n, ref in enumerate((r0, r1, r2, r3)):
        got[2 * n : 2 * n + 2] = ref[...]

    def body(x, carry):
        out[x] = new[x]
        return carry

    lax.fori_loop(0, CX, body, 0, unroll=8)
    lane = lax.broadcasted_iota(jnp.int32, (BC, BC, NZ), 2)
    iotas = box_iotas()

    def entry(k, carry):
        @pl.when(meta[k] >= 0)
        def _():
            at = (pl.ds(meta[4 + k], BC), pl.ds(pl.multiple_of(meta[8 + k], 16), BC))
            moved = moved_box(meta, got, k, *iotas)
            oz = meta[12 + k]
            out[at[0], at[1], :] = jnp.where(
                (lane >= oz) & (lane < oz + BC), moved, out[at[0], at[1], :]
            )

        return carry

    lax.fori_loop(0, MOST, entry, 0)

    def plane(y):
        return out.reshape(CX * CY, NZ)[pl.ds(y, CX, stride=CY), :]

    xup[...] = out[CX - 2 : CX]
    xdn[...] = out[0:2]
    yup[0:64, :] = plane(CY - 2)
    yup[64:128, :] = plane(CY - 1)
    ydn[0:64, :] = plane(0)
    ydn[64:128, :] = plane(1)
    yup[128:136, :] = jnp.zeros((8, NZ), F32)
    ydn[128:136, :] = jnp.zeros((8, NZ), F32)


def insert(meta, new, received):
    x = jax.ShapeDtypeStruct((2, CY, NZ), F32)
    y = jax.ShapeDtypeStruct((2 * CX + 8, NZ), F32)
    return pl.pallas_call(
        insert_kernel,
        out_shape=(jax.ShapeDtypeStruct(BLOCK, F32), x, x, y, y),
        in_specs=[SMEM] + [VMEM] * 5,
        out_specs=[VMEM] * 5,
        scratch_shapes=[pltpu.VMEM((8, BC, BC * BC), F32)],
        compiler_params=pltpu.CompilerParams(vmem_limit_bytes=LIMIT),
        name="insert",
    )(meta, new, *received)


def emit_kernel(new, f, g, new_out, f_out, g_out, sem):
    ends = ((new, new_out), (f, f_out), (g, g_out))
    copies = [pltpu.make_async_copy(*pair, sem.at[n]) for n, pair in enumerate(ends)]
    for copy in copies:
        copy.start()
    for copy in copies:
        copy.wait()


def emit(new, f, g):
    box = jax.ShapeDtypeStruct((2, FINE, PLANE), F32)
    return pl.pallas_call(
        emit_kernel,
        out_shape=(jax.ShapeDtypeStruct(BLOCK, F32), box, box),
        in_specs=[VMEM] * 3,
        out_specs=[HBM] * 3,
        scratch_shapes=[pltpu.SemaphoreType.DMA((3,))],
        compiler_params=pltpu.CompilerParams(vmem_limit_bytes=LIMIT),
        cost_estimate=pl.CostEstimate(flops=0, bytes_accessed=9000000, transcendentals=0),
        name="emit",
    )(new, f, g)


def finish_kernel(meta, new, written, r0, r1, r2, r3, out, got, boxes, sem):
    def region(k):
        return pl.ds(meta[4 + k], BC), pl.ds(pl.multiple_of(meta[8 + k], 16), BC)

    def store(k):
        x, y = region(k)
        return pltpu.make_async_copy(boxes.at[k], out.at[x, y, :], sem.at[k])

    slots = []
    for k in range(MOST):
        slot = k
        for n in reversed(range(k)):
            same = (meta[4 + n] == meta[4 + k]) & (meta[8 + n] == meta[8 + k]) & (meta[n] >= 0)
            slot = jnp.where(same, n, slot)
        slots.append(slot)
    for n, ref in enumerate((r0, r1, r2, r3)):
        got[2 * n : 2 * n + 2] = ref[...]
    lane = lax.broadcasted_iota(jnp.int32, (BC, BC, NZ), 2)
    iotas = box_iotas()
    for k in range(MOST):

        @pl.when(meta[k] >= 0)
        def _():
            slot = slots[k]

            @pl.when(slot == k)
            def _():
                x, y = region(k)
                boxes[k] = new[x, y, :]

            moved = moved_box(meta, got, k, *iotas)
            oz = meta[12 + k]
            boxes[slot] = jnp.where((lane >= oz) & (lane < oz + BC), moved, boxes[slot])

    for k in range(MOST):

        @pl.when((meta[k] >= 0) & (slots[k] == k))
        def _():
            store(k).start()

    for k in range(MOST):

        @pl.when((meta[k] >= 0) & (slots[k] == k))
        def _():
            store(k).wait()


def finish(meta, new, written, received):
    return pl.pallas_call(
        finish_kernel,
        out_shape=jax.ShapeDtypeStruct(BLOCK, F32),
        in_specs=[SMEM, VMEM, ANY] + [VMEM] * 4,
        out_specs=ANY,
        input_output_aliases={2: 0},
        scratch_shapes=[
            pltpu.VMEM((8, BC, BC * BC), F32),
            pltpu.VMEM((MOST, BC, BC, NZ), F32),
            pltpu.SemaphoreType.DMA((MOST,)),
        ],
        compiler_params=pltpu.CompilerParams(vmem_limit_bytes=LIMIT),
        name="finish",
    )(meta, new, written, *received)


def ring(size, by):
    return [(i, (i + by) % size) for i in range(size)]


def halo(meta, xup, xdn, yup, ydn):
    xlo = lax.ppermute(xup, "tile", ring(8, 1))
    xhi = lax.ppermute(xdn, "tile", ring(8, -1))
    yup, ydn = corners(meta, yup, ydn, xlo, xhi)
    ylo = lax.ppermute(yup, "bulk", ring(16, 1))
    yhi = lax.ppermute(ydn, "bulk", ring(16, -1))
    return xlo, xhi, ylo, yhi


def trade(values):
    done = [values[0]]
    for value, away in zip(values[1:], (1, 64, 65)):
        done.append(lax.ppermute(value, ("tile", "bulk"), [(d, d ^ away) for d in range(128)]))
    return done


def on_device(
    coarse_now,
    coarse_before,
    coarse_courant,
    coarse_absorb,
    fine_now,
    fine_before,
    fine_courant,
    fine_absorb,
    box_anchor,
    intersection,
):
    place = jnp.stack([lax.axis_index("tile"), lax.axis_index("bulk")]).astype(jnp.int32)
    meta = jnp.concatenate([intersection.reshape(16), box_anchor.reshape(6), place])
    consts = tables()
    inputs = (coarse_now, coarse_before, coarse_courant, coarse_absorb)
    extras = halo(meta, *x_edges(*inputs), *y_edges(*inputs))
    weights = factors(fine_courant, fine_absorb)
    first = ahead(fine_now, fine_before, weights, consts[0])
    raw, two, side, start = first_inner(*inputs)
    new, *faces = coarse(True, meta, start, raw, side, extras, extras)
    f, g, res = fine(meta, fine_now, first, weights, trade(faces), consts)
    middle, *packed = insert(meta, new, trade([res] * 4))
    first = ahead(f, g, weights, consts[0])
    halos = halo(meta, *packed)
    raw, q = second_inner(middle, start, two, side)
    new, *faces = coarse(False, meta, middle, raw, side, halos, extras)
    f, g, res = fine(meta, f, first, weights, trade(faces), consts)
    written, f, g = emit(new, f, g)
    p = finish(meta, new, written, trade([res] * 4))
    return p, q, f, g


def solution(mesh):
    grid = P("tile", "bulk", None)
    boxes = P(("tile", "bulk"), None, None)
    in_specs = (grid,) * 4 + (boxes,) * 4 + (P(("tile", "bulk"), None), boxes)
    return jax.shard_map(
        on_device, mesh=mesh, in_specs=in_specs, out_specs=(grid, grid, boxes, boxes), check_vma=False
    )
```

```python
import functools

import jax
import jax.numpy as jnp
import numpy as np
from jax import lax
from jax.experimental import pallas as pl
from jax.experimental.pallas import tpu as pltpu
from jax.sharding import PartitionSpec as P

CX = 64
CY = 64
NZ = 128
BC = 16
FINE = 48
PLANE = FINE * FINE
MOST = 4
F32 = jnp.float32
BF16 = jnp.bfloat16
ANY = pl.BlockSpec(memory_space=pl.ANY)
HBM = pl.BlockSpec(memory_space=pltpu.HBM)
VMEM = pl.BlockSpec(memory_space=pltpu.VMEM)
SMEM = pl.BlockSpec(memory_space=pltpu.SMEM)
LIMIT = 20 * 1024 * 1024


def tables():
    flat = np.arange(PLANE)
    y, z = flat // FINE, flat % FINE
    masks = np.stack([z > 0, z < FINE - 1]).astype(np.float32)
    masks = np.repeat(masks[:, None, :384], 8, axis=1)
    r = np.arange(BC)[:, None]
    spread = np.zeros((128, PLANE), np.float32)
    spread[0:16] = (y == 0) & (z // 3 == r)
    spread[16:32] = (y == FINE - 1) & (z // 3 == r)
    spread[32:48] = (z == 0) & (y // 3 == r)
    spread[48:64] = (z == FINE - 1) & (y // 3 == r)
    spread[64:80] = z // 3 == r
    spread[80:96] = z // 3 == r
    spread = np.concatenate([spread, spread], axis=0)
    pick = (y // 3 == r).astype(np.float32)
    pool = ((y // 3 * BC + z // 3)[:, None] == np.arange(BC * BC)[None, :]).astype(np.float32)
    return jnp.asarray(masks), jnp.asarray(spread, BF16), jnp.asarray(pick), jnp.asarray(pool, BF16)


def partner_of(meta, device):
    away = (meta[22] * 16 + meta[23]) ^ device
    return (away & 1) + 2 * ((away >> 6) & 1)


def far(value):
    return pltpu.with_memory_space_constraint(value, pltpu.HBM)


def split(value):
    high = value.astype(BF16)
    low = (value - high.astype(F32)).astype(BF16)
    return high, low


def dot(left, right):
    return jnp.dot(left, right, preferred_element_type=F32)


def x_edges_kernel(p, q, c, a, xup, xdn, sem):
    ends = [(p.at[CX - 2 : CX], xup.at[0:2]), (p.at[0:2], xdn.at[0:2])]
    for n, ref in enumerate((q, c, a)):
        ends.append((ref.at[CX - 1], xup.at[n + 2]))
        ends.append((ref.at[0], xdn.at[n + 2]))
    copies = [pltpu.make_async_copy(*pair, sem.at[n]) for n, pair in enumerate(ends)]
    for copy in copies:
        copy.start()
    for copy in copies:
        copy.wait()


def x_edges(p, q, c, a):
    x = jax.ShapeDtypeStruct((5, CY, NZ), F32)
    return pl.pallas_call(
        x_edges_kernel,
        out_shape=(x, x),
        in_specs=[HBM] * 4,
        out_specs=[VMEM] * 2,
        scratch_shapes=[pltpu.SemaphoreType.DMA((8,))],
        compiler_params=pltpu.CompilerParams(vmem_limit_bytes=LIMIT),
        name="x_edges",
    )(*[far(v) for v in (p, q, c, a)])


def y_edges_kernel(p, q, c, a, yup, ydn, tiles, sem):
    ends = []
    for n, ref in enumerate((p, q, c, a)):
        ends.append((ref.at[:, CY - 8 : CY, :], tiles.at[0, n]))
        ends.append((ref.at[:, 0:8, :], tiles.at[1, n]))
    copies = [pltpu.make_async_copy(*pair, sem.at[n]) for n, pair in enumerate(ends)]
    for copy in copies:
        copy.start()
    for copy in copies:
        copy.wait()

    def plane(side, n, y):
        return tiles.at[side, n].reshape(CX * 8, NZ)[pl.ds(y, CX, stride=8), :]

    yup[0:64, :] = plane(0, 0, 6)
    yup[64:128, :] = plane(0, 0, 7)
    ydn[0:64, :] = plane(1, 0, 0)
    ydn[64:128, :] = plane(1, 0, 1)
    for n in range(1, 4):
        yup[64 * (n + 1) : 64 * (n + 2), :] = plane(0, n, 7)
        ydn[64 * (n + 1) : 64 * (n + 2), :] = plane(1, n, 0)
    yup[320:328, :] = jnp.zeros((8, NZ), F32)
    ydn[320:328, :] = jnp.zeros((8, NZ), F32)


def y_edges(p, q, c, a):
    y = jax.ShapeDtypeStruct((5 * CX + 8, NZ), F32)
    return pl.pallas_call(
        y_edges_kernel,
        out_shape=(y, y),
        in_specs=[HBM] * 4,
        out_specs=[VMEM] * 2,
        scratch_shapes=[pltpu.VMEM((2, 4, CX, 8, NZ), F32), pltpu.SemaphoreType.DMA((8,))],
        compiler_params=pltpu.CompilerParams(vmem_limit_bytes=LIMIT),
        cost_estimate=pl.CostEstimate(flops=0, bytes_accessed=5000000, transcendentals=0),
        name="y_edges",
    )(*[far(v) for v in (p, q, c, a)])


def corners_kernel(base, meta, yup, ydn, xlo, xhi, yup_out, ydn_out, rows, sem):
    lo = meta[22] > 0
    hi = meta[22] < 7
    for n, y in ((0, CY - 1), (1, 0)):
        rows[n, 0:1, :] = jnp.where(lo, xlo[1, y : y + 1, :], 0.0)
        rows[n, 1:2, :] = jnp.where(hi, xhi[0, y : y + 1, :], 0.0)
    copies = [
        pltpu.make_async_copy(rows.at[0], yup_out.at[base : base + 8, :], sem.at[0]),
        pltpu.make_async_copy(rows.at[1], ydn_out.at[base : base + 8, :], sem.at[1]),
    ]
    for copy in copies:
        copy.start()
    for copy in copies:
        copy.wait()


def corners(meta, yup, ydn, xlo, xhi):
    base = yup.shape[0] - 8
    y = jax.ShapeDtypeStruct(yup.shape, F32)
    return pl.pallas_call(
        functools.partial(corners_kernel, base),
        out_shape=(y, y),
        in_specs=[SMEM, ANY, ANY, VMEM, VMEM],
        out_specs=[ANY, ANY],
        input_output_aliases={1: 0, 2: 1},
        scratch_shapes=[pltpu.VMEM((2, 8, NZ), F32), pltpu.SemaphoreType.DMA((2,))],
        compiler_params=pltpu.CompilerParams(vmem_limit_bytes=LIMIT),
        name="corners",
    )(meta, yup, ydn, xlo, xhi)


def inverse(value):
    guess = pl.reciprocal(value, approx=True)
    guess = guess * (2.0 - value * guess)
    return guess * (2.0 - value * guess)


def lanes_both_ways(here):
    lane = lax.broadcasted_iota(jnp.int32, here.shape, 1)
    before = jnp.where(lane > 0, pltpu.roll(here, 1, 1), 0.0)
    after = jnp.where(lane < NZ - 1, pltpu.roll(here, NZ - 1, 1), 0.0)
    return before + after


def advance(here, beside, before, courant, absorb):
    inv = inverse(1.0 + absorb)
    return before + (2.0 * inv) * (here - before) + (courant * inv) * (beside - 6.0 * here)


CHUNKS = 4
ROWS = CX // CHUNKS
BLOCK = (CX, CY, NZ)
PADDED = (CX + 2, CY + 16, NZ)


def clear_rim(pe):
    edge = jnp.zeros((CX, 8, NZ), F32)
    pe[1 : CX + 1, 0:8, :] = edge
    pe[1 : CX + 1, CY + 8 : CY + 16, :] = edge
    pe[0] = jnp.zeros((CY + 16, NZ), F32)
    pe[CX + 1] = jnp.zeros((CY + 16, NZ), F32)


def around(pe, x):
    here = pe[x + 1, 8 : CY + 8, :]
    beside = pe[x, 8 : CY + 8, :] + pe[x + 2, 8 : CY + 8, :]
    beside = beside + pe[x + 1, 7 : CY + 7, :] + pe[x + 1, 9 : CY + 9, :]
    return here, beside + lanes_both_ways(here)


def first_inner_kernel(p, q, c, a, raw, two, side, here_out, pe, qs, cs, as_, sem):
    copies = []
    for n in range(CHUNKS):
        s = slice(ROWS * n, ROWS * n + ROWS)
        to_rows = slice(1 + ROWS * n, 1 + ROWS * n + ROWS)
        part = [pltpu.make_async_copy(p.at[s], pe.at[to_rows, 8 : CY + 8, :], sem.at[0, n])]
        for m, (ref, to) in enumerate(((q, qs), (c, cs), (a, as_))):
            part.append(pltpu.make_async_copy(ref.at[s], to.at[s], sem.at[m + 1, n]))
        copies.append(part)
    for part in copies:
        for copy in part:
            copy.start()
    clear_rim(pe)
    copies[0][0].wait()

    def body(x, carry):
        here, beside = around(pe, x)
        inv = inverse(1.0 + as_[x])
        twice = 2.0 * inv
        weight = cs[x] * inv
        two[x] = twice
        side[x] = weight
        here_out[x] = here
        raw[x] = qs[x] + twice * (here - qs[x]) + weight * (beside - 6.0 * here)
        return carry

    for n in range(CHUNKS):
        if n + 1 < CHUNKS:
            copies[n + 1][0].wait()
        for copy in copies[n][1:]:
            copy.wait()
        lax.fori_loop(ROWS * n, ROWS * n + ROWS, body, 0, unroll=8)


def first_inner(p, q, c, a):
    block = jax.ShapeDtypeStruct(BLOCK, F32)
    return pl.pallas_call(
        first_inner_kernel,
        out_shape=(block, block, block, block),
        in_specs=[HBM] * 4,
        out_specs=[VMEM] * 4,
        scratch_shapes=[
            pltpu.VMEM(PADDED, F32),
            pltpu.VMEM(BLOCK, F32),
            pltpu.VMEM(BLOCK, F32),
            pltpu.VMEM(BLOCK, F32),
            pltpu.SemaphoreType.DMA((4, CHUNKS)),
        ],
        compiler_params=pltpu.CompilerParams(vmem_limit_bytes=LIMIT),
        cost_estimate=pl.CostEstimate(flops=12000000, bytes_accessed=10000000, transcendentals=0),
        name="first_inner",
    )(*[far(v) for v in (p, q, c, a)])


def second_inner_kernel(p, q, two, side, raw, out, pe, sem):
    store = pltpu.make_async_copy(p, out, sem)
    store.start()
    clear_rim(pe)

    def fill(x, carry):
        pe[x + 1, 8 : CY + 8, :] = p[x]
        return carry

    lax.fori_loop(0, CX, fill, 0, unroll=8)

    def body(x, carry):
        here, beside = around(pe, x)
        raw[x] = q[x] + two[x] * (here - q[x]) + side[x] * (beside - 6.0 * here)
        return carry

    lax.fori_loop(0, CX, body, 0, unroll=8)
    store.wait()


def second_inner(p, q, two, side):
    return pl.pallas_call(
        second_inner_kernel,
        out_shape=(jax.ShapeDtypeStruct(BLOCK, F32),) * 2,
        in_specs=[VMEM] * 4,
        out_specs=[VMEM, ANY],
        scratch_shapes=[pltpu.VMEM(PADDED, F32), pltpu.SemaphoreType.DMA],
        compiler_params=pltpu.CompilerParams(vmem_limit_bytes=LIMIT),
        cost_estimate=pl.CostEstimate(flops=12000000, bytes_accessed=8000000, transcendentals=0),
        name="second_inner",
    )(p, q, two, side)


def coarse_kernel(
    first,
    meta,
    p,
    raw,
    weight,
    pxlo,
    pxhi,
    pylo,
    pyhi,
    exlo,
    exhi,
    eylo,
    eyhi,
    new,
    face0,
    face1,
    face2,
    face3,
    rim,
    ring,
    faces,
):
    tile, bulk = meta[22], meta[23]
    inside_grid = (tile > 0, tile < 7, bulk > 0, bulk < 15)
    base = pylo.shape[0] - 8
    qlo, qhi = (2, 2) if first else (1, 0)

    def keep(n, value):
        return jnp.where(inside_grid[n], value, 0.0)

    def body(x, carry):
        new[x] = raw[x]
        return carry

    lax.fori_loop(0, CX, body, 0, unroll=8)

    def plane(ref, y):
        return ref.reshape(CX * CY, NZ)[pl.ds(y, CX, stride=CY), :]

    def corner(n, ref, at):
        return keep(n, ref[base + at : base + at + 1, :])

    def extra(ref, n):
        return ref[n] if len(ref.shape) == 3 else ref[64 * n : 64 * n + 64, :]

    sides = (
        (pxlo[1], pxlo[0], p[0], corner(2, pylo, 0), corner(3, pyhi, 0), exlo, qlo),
        (pxhi[0], pxhi[1], p[CX - 1], corner(2, pylo, 1), corner(3, pyhi, 1), exhi, qhi),
        (pylo[64:128, :], pylo[0:64, :], plane(p, 0), *[pylo[base + n : base + n + 1, :] for n in (0, 1)], eylo, qlo),
        (pyhi[0:64, :], pyhi[64:128, :], plane(p, CY - 1), *[pyhi[base + n : base + n + 1, :] for n in (0, 1)], eyhi, qhi),
    )
    for n, (here, out, inside, before, after, ref, at_q) in enumerate(sides):
        here = keep(n, here)
        rim[0, n] = here
        ring[n, 7:8, :] = keep(n, before)
        ring[n, 8:72, :] = here
        ring[n, 72:73, :] = keep(n, after)
        beside = ring[n, 7:71, :] + ring[n, 9:73, :] + keep(n, out) + inside + lanes_both_ways(here)
        rim[1, n] = advance(here, beside, *[keep(n, extra(ref, m)) for m in (at_q, 3, 4)])

    new[0] = new[0] + weight[0] * rim[0, 0]
    new[CX - 1] = new[CX - 1] + weight[CX - 1] * rim[0, 1]
    low = (plane(weight, 0) * rim[0, 2])[:, None, :]
    new[:, 0:1, :] = new[:, 0:1, :] + low
    high = (plane(weight, CY - 1) * rim[0, 3])[:, None, :]
    new[:, CY - 1 : CY, :] = new[:, CY - 1 : CY, :] + high

    from_z = lax.broadcasted_iota(jnp.int32, (NZ, NZ), 0)
    to_lane = lax.broadcasted_iota(jnp.int32, (NZ, NZ), 1)
    out_lane = lax.broadcasted_iota(jnp.int32, (BC, NZ), 1)
    deep_lane = lax.broadcasted_iota(jnp.int32, (BC, BC, NZ), 2)
    deep_y = lax.broadcasted_iota(jnp.int32, (BC, BC, NZ), 1)
    diagonal = (deep_lane & 15) == deep_y

    def entry(k, carry):
        ident = meta[k]

        @pl.when(ident >= 0)
        def _():
            ox = pl.multiple_of(meta[4 + k], 16)
            oy = pl.multiple_of(meta[8 + k], 16)
            oz = meta[12 + k]
            where_to = partner_of(meta, ident >> 1) * 2 + (ident & 1)
            low_face = (to_lane >= 32) & (to_lane < 48)
            high_face = (to_lane >= 48) & (to_lane < 64)
            source = jnp.where(
                low_face, oz - 1, jnp.where(high_face, oz + BC, oz + (to_lane & 15))
            )
            mover = jnp.where(from_z == source, 1.0, 0.0).astype(BF16)
            mover = jnp.concatenate([mover, mover], axis=0)
            for t, ref in enumerate((p, new)):
                cube = ref[pl.ds(ox, BC), pl.ds(oy, BC), :].reshape(BC * BC, NZ)
                y = pl.multiple_of(jnp.maximum(oy - 8, 0), 8)
                ym = ref[pl.ds(ox, BC), pl.ds(y, 8), :][:, 7, :]
                ym = jnp.where(oy == 0, rim[t, 2, pl.ds(ox, BC), :], ym)
                y = pl.multiple_of(jnp.minimum(oy + BC, CY - 8), 8)
                yp = ref[pl.ds(ox, BC), pl.ds(y, 8), :][:, 0, :]
                yp = jnp.where(oy == CY - BC, rim[t, 3, pl.ds(ox, BC), :], yp)
                xm = ref[jnp.maximum(ox - 1, 0), pl.ds(oy, BC), :]
                xm = jnp.where(ox == 0, rim[t, 0, pl.ds(oy, BC), :], xm)
                xp = ref[jnp.minimum(ox + BC, CX - 1), pl.ds(oy, BC), :]
                xp = jnp.where(ox == CX - BC, rim[t, 1, pl.ds(oy, BC), :], xp)
                high, low = split(jnp.concatenate([cube, ym, yp, xm, xp], axis=0))
                moved = dot(jnp.concatenate([high, low], axis=1), mover)
                z_face = jnp.where(diagonal, moved[0:256].reshape(BC, BC, NZ), 0.0).sum(axis=1)
                tile_ = jnp.where(out_lane < 80, moved[288:304], moved[304:320])
                tile_ = jnp.where(out_lane < 64, z_face, tile_)
                tile_ = jnp.where(out_lane < 32, moved[272:288], tile_)
                tile_ = jnp.where(out_lane < 16, moved[256:272], tile_)
                faces[where_to, t] = tile_

        return carry

    lax.fori_loop(0, MOST, entry, 0)
    for n, ref in enumerate((face0, face1, face2, face3)):
        ref[...] = faces[2 * n : 2 * n + 2]


def coarse(first, meta, p, raw, weight, halos, extras):
    face = jax.ShapeDtypeStruct((2, 2, BC, NZ), F32)
    return pl.pallas_call(
        functools.partial(coarse_kernel, first),
        out_shape=(jax.ShapeDtypeStruct(BLOCK, F32), face, face, face, face),
        in_specs=[SMEM] + [VMEM] * 11,
        out_specs=[VMEM] * 5,
        scratch_shapes=[
            pltpu.VMEM((2, 4, 64, NZ), F32),
            pltpu.VMEM((4, 80, NZ), F32),
            pltpu.VMEM((8, 2, BC, NZ), F32),
        ],
        compiler_params=pltpu.CompilerParams(vmem_limit_bytes=LIMIT),
        name="coarse",
    )(meta, p, raw, weight, *halos, *extras)


def factors_kernel(c, a, one, two, three, cs, as_, sem):
    copies = []
    for j in range(2):
        copies.append(pltpu.make_async_copy(c.at[j], cs.at[j], sem.at[2 * j]))
        copies.append(pltpu.make_async_copy(a.at[j], as_.at[j], sem.at[2 * j + 1]))
    for copy in copies:
        copy.start()
    for j in range(2):
        copies[2 * j].wait()
        copies[2 * j + 1].wait()

        def body(i, carry):
            s = pl.ds(pl.multiple_of(8 * i, 8), 8)
            inv = inverse(1.0 + as_[j, s, :])
            side = cs[j, s, :] * inv
            three[j, s, :] = side
            one[j, s, :] = 2.0 * inv - 6.0 * side
            two[j, s, :] = 1.0 - 2.0 * inv
            return carry

        lax.fori_loop(0, FINE // 8, body, 0)


def factors(c, a):
    box = jax.ShapeDtypeStruct((2, FINE, PLANE), F32)
    return pl.pallas_call(
        factors_kernel,
        out_shape=(box, box, box),
        in_specs=[HBM] * 2,
        out_specs=[VMEM] * 3,
        scratch_shapes=[pltpu.VMEM(box.shape, F32)] * 2 + [pltpu.SemaphoreType.DMA((4,))],
        compiler_params=pltpu.CompilerParams(vmem_limit_bytes=LIMIT),
        cost_estimate=pl.CostEstimate(flops=3000000, bytes_accessed=4000000, transcendentals=0),
        name="factors",
    )(far(c), far(a))


def turned(v):
    return {d: (pltpu.roll(v, d, 1), pltpu.roll(v, 128 - d, 1)) for d in (1, 48)}


def beside_in_plane(row, masks):
    small = lax.broadcasted_iota(jnp.int32, (8, 128), 1)
    zero = jnp.zeros((8, 128), F32)
    none = {d: (zero, zero) for d in (1, 48)}
    cur = row(0)
    cur_t = turned(cur)
    before_t = none
    masks = [[masks[n, :, 128 * r : 128 * r + 128] for r in range(3)] for n in range(2)]
    for k in range(PLANE // 128):
        ls = slice(128 * k, 128 * k + 128)
        last = k + 1 == PLANE // 128
        nxt = cur if last else row(k + 1)
        nxt_t = none if last else turned(nxt)
        total = jnp.where(small < 48, before_t[48][0], cur_t[48][0])
        total = total + jnp.where(small >= 80, nxt_t[48][1], cur_t[48][1])
        down = jnp.where(small < 1, before_t[1][0], cur_t[1][0])
        up = jnp.where(small >= 127, nxt_t[1][1], cur_t[1][1])
        total = total + down * masks[0][k % 3] + up * masks[1][k % 3]
        yield ls, cur, total
        before_t, cur, cur_t = cur_t, nxt, nxt_t


def ahead_kernel(f, g, one, two, three, masks, raw, buf, sem):
    copies = [pltpu.make_async_copy(f.at[j], buf.at[j, 8:56, :], sem.at[j]) for j in range(2)]
    for copy in copies:
        copy.start()
    for j in range(2):
        buf[j, 0:8, :] = jnp.zeros((8, PLANE), F32)
        buf[j, 56:64, :] = jnp.zeros((8, PLANE), F32)
    for copy in copies:
        copy.wait()

    def box(j, carry):
        for i in range(6):
            s = slice(8 * i, 8 * i + 8)

            def row(k):
                return buf[j, 8 + 8 * i : 16 + 8 * i, 128 * k : 128 * k + 128]

            for ls, cur, total in beside_in_plane(row, masks):
                total = total + buf[j, 7 + 8 * i : 15 + 8 * i, ls] + buf[j, 9 + 8 * i : 17 + 8 * i, ls]
                raw[j, s, ls] = (
                    one[j, s, ls] * cur + two[j, s, ls] * g[j, s, ls] + three[j, s, ls] * total
                )
        return carry

    lax.fori_loop(0, 2, box, 0)


def ahead(f, g, weights, masks):
    box = jax.ShapeDtypeStruct((2, FINE, PLANE), F32)
    return pl.pallas_call(
        ahead_kernel,
        out_shape=box,
        in_specs=[ANY] + [VMEM] * 5,
        out_specs=VMEM,
        scratch_shapes=[pltpu.VMEM((2, 64, PLANE), F32), pltpu.SemaphoreType.DMA((2,))],
        compiler_params=pltpu.CompilerParams(vmem_limit_bytes=LIMIT),
        cost_estimate=pl.CostEstimate(flops=5000000, bytes_accessed=5000000, transcendentals=0),
        name="ahead",
    )(f, g, *weights, masks)


def fine_kernel(
    meta,
    f,
    raw,
    one,
    two,
    three,
    r0,
    r1,
    r2,
    r3,
    masks,
    spread,
    pick,
    pool,
    f_out,
    g_out,
    res,
    buf,
    ghost,
    xrow,
    faces,
):
    for n, ref in enumerate((r0, r1, r2, r3)):
        faces[2 * n : 2 * n + 2] = ref[...]

    lane = lax.broadcasted_iota(jnp.int32, (BC, NZ), 1)
    wide_lane = jnp.concatenate([lane, lane], axis=1)
    tall = lax.broadcasted_iota(jnp.int32, (FINE, BC), 0)
    wide = lax.broadcasted_iota(jnp.int32, (FINE, BC), 1)
    thrice = jnp.where((tall >= 3 * wide) & (tall < 3 * wide + 3), 1.0, 0.0).astype(BF16)
    sides, rows = [], []
    for j in range(2):
        source = (meta[16 + 3 * j] >> 6) * 16 + (meta[17 + 3 * j] >> 6)
        at = partner_of(meta, source) * 2 + j
        old = jnp.where(lane < 96, faces[at, 0], 0.0)
        new = jnp.where(lane < 96, faces[at, 1], 0.0)
        for m in range(3):
            high, low = split(old + (m / 3.0) * (new - old))
            both = jnp.concatenate([high, low], axis=1)
            zero = jnp.zeros_like(both)
            sides.append(jnp.where(wide_lane < 64, both, zero))
            rows.append(jnp.where((wide_lane >= 64) & (wide_lane < 80), both, zero))
            rows.append(jnp.where(wide_lane >= 80, both, zero))
    tall_sides = dot(thrice, jnp.concatenate(sides, axis=1)).astype(BF16)
    sides = [tall_sides[:, 256 * n : 256 * n + 256] for n in range(6)]
    spreaded = dot(jnp.concatenate(sides + rows, axis=0), spread[...])
    for j in range(2):
        for m in range(3):
            at = 48 * (3 * j + m)
            ghost[m, j] = spreaded[at : at + 48]
        for n in range(6):
            at = 288 + 16 * (6 * j + n)
            part = spreaded[at : at + 16] * pick[...]
            xrow[j, n : n + 1, :] = part.sum(axis=0, keepdims=True)

    def first(j):
        for i in range(6):
            s = slice(8 * i, 8 * i + 8)
            buf[0, j, 8 + 8 * i : 16 + 8 * i, :] = raw[j, s, :] + three[j, s, :] * ghost[0, j, s, :]
        for n, x in ((0, 0), (1, FINE - 1)):
            buf[0, j, 8 + x : 9 + x, :] = (
                buf[0, j, 8 + x : 9 + x, :] + three[j, x : x + 1, :] * xrow[j, n : n + 1, :]
            )

    def substep(m, j):
        buf[m - 1, j, 7:8, :] = xrow[j, 2 * m : 2 * m + 1, :]
        buf[m - 1, j, 56:57, :] = xrow[j, 2 * m + 1 : 2 * m + 2, :]
        for i in range(6):
            s = slice(8 * i, 8 * i + 8)
            pad = slice(8 + 8 * i, 16 + 8 * i)

            def row(k):
                return buf[m - 1, j, pad, 128 * k : 128 * k + 128]

            for ls, cur, total in beside_in_plane(row, masks):
                total = total + ghost[m, j, s, ls]
                total = total + (
                    buf[m - 1, j, 7 + 8 * i : 15 + 8 * i, ls]
                    + buf[m - 1, j, 9 + 8 * i : 17 + 8 * i, ls]
                )
                old = f[j, s, ls] if m == 1 else buf[0, j, pad, ls]
                value = one[j, s, ls] * cur + two[j, s, ls] * old + three[j, s, ls] * total
                if m == 1:
                    buf[1, j, pad, ls] = value
                    g_out[j, s, ls] = value
                else:
                    f_out[j, s, ls] = value

    def box(j, carry):
        first(j)
        substep(1, j)
        substep(2, j)
        return carry

    lax.fori_loop(0, 2, box, 0, unroll=True)
    tall = lax.broadcasted_iota(jnp.int32, (BC, FINE), 1)
    wide = lax.broadcasted_iota(jnp.int32, (BC, FINE), 0)
    gather = jnp.where((tall >= 3 * wide) & (tall < 3 * wide + 3), 1.0, 0.0).astype(BF16)
    parts = [part for j in range(2) for part in split(f_out[j])]
    pooled = dot(jnp.concatenate(parts, axis=0), pool[...])
    parts = []
    for j in range(2):
        parts += split(pooled[96 * j : 96 * j + 48] + pooled[96 * j + 48 : 96 * j + 96])
    means = dot(gather, jnp.concatenate(parts, axis=1))
    for j in range(2):
        at = 512 * j
        res[j] = (means[:, at : at + 256] + means[:, at + 256 : at + 512]) * (1.0 / 27.0)


def fine(meta, f, raw, weights, received, consts):
    box = jax.ShapeDtypeStruct((2, FINE, PLANE), F32)
    return pl.pallas_call(
        fine_kernel,
        out_shape=(box, box, jax.ShapeDtypeStruct((2, BC, BC * BC), F32)),
        in_specs=[SMEM] + [VMEM] * 13,
        out_specs=[VMEM] * 3,
        scratch_shapes=[
            pltpu.VMEM((2, 2, 64, PLANE), F32),
            pltpu.VMEM((3, 2, FINE, PLANE), F32),
            pltpu.VMEM((2, 8, PLANE), F32),
            pltpu.VMEM((8, 2, BC, NZ), F32),
        ],
        compiler_params=pltpu.CompilerParams(vmem_limit_bytes=LIMIT),
        name="fine",
    )(meta, f, raw, *weights, *received, *consts)


def moved_box(meta, got, k, mine, from_yz, to_lane):
    ident = meta[k]
    value = got[partner_of(meta, ident >> 1) * 2 + (ident & 1)]
    full = jnp.where(mine, value[:, None, :], 0.0).reshape(BC * BC, BC * BC)
    high, low = split(full)
    mover = jnp.where(to_lane == meta[12 + k] + (from_yz & 15), 1.0, 0.0).astype(BF16)
    moved = dot(jnp.concatenate([high, low], axis=1), jnp.concatenate([mover, mover], axis=0))
    return moved.reshape(BC, BC, NZ)


def box_iotas():
    y_of = lax.broadcasted_iota(jnp.int32, (BC, BC, BC * BC), 1)
    lane_of = lax.broadcasted_iota(jnp.int32, (BC, BC, BC * BC), 2)
    from_yz = lax.broadcasted_iota(jnp.int32, (BC * BC, NZ), 0)
    to_lane = lax.broadcasted_iota(jnp.int32, (BC * BC, NZ), 1)
    return (lane_of >> 4) == y_of, from_yz, to_lane


def insert_kernel(meta, new, r0, r1, r2, r3, out, xup, xdn, yup, ydn, got):
    for n, ref in enumerate((r0, r1, r2, r3)):
        got[2 * n : 2 * n + 2] = ref[...]

    def body(x, carry):
        out[x] = new[x]
        return carry

    lax.fori_loop(0, CX, body, 0, unroll=8)
    lane = lax.broadcasted_iota(jnp.int32, (BC, BC, NZ), 2)
    iotas = box_iotas()

    def entry(k, carry):
        @pl.when(meta[k] >= 0)
        def _():
            at = (pl.ds(meta[4 + k], BC), pl.ds(pl.multiple_of(meta[8 + k], 16), BC))
            moved = moved_box(meta, got, k, *iotas)
            oz = meta[12 + k]
            out[at[0], at[1], :] = jnp.where(
                (lane >= oz) & (lane < oz + BC), moved, out[at[0], at[1], :]
            )

        return carry

    lax.fori_loop(0, MOST, entry, 0)

    def plane(y):
        return out.reshape(CX * CY, NZ)[pl.ds(y, CX, stride=CY), :]

    xup[...] = out[CX - 2 : CX]
    xdn[...] = out[0:2]
    yup[0:64, :] = plane(CY - 2)
    yup[64:128, :] = plane(CY - 1)
    ydn[0:64, :] = plane(0)
    ydn[64:128, :] = plane(1)
    yup[128:136, :] = jnp.zeros((8, NZ), F32)
    ydn[128:136, :] = jnp.zeros((8, NZ), F32)


def insert(meta, new, received):
    x = jax.ShapeDtypeStruct((2, CY, NZ), F32)
    y = jax.ShapeDtypeStruct((2 * CX + 8, NZ), F32)
    return pl.pallas_call(
        insert_kernel,
        out_shape=(jax.ShapeDtypeStruct(BLOCK, F32), x, x, y, y),
        in_specs=[SMEM] + [VMEM] * 5,
        out_specs=[VMEM] * 5,
        scratch_shapes=[pltpu.VMEM((8, BC, BC * BC), F32)],
        compiler_params=pltpu.CompilerParams(vmem_limit_bytes=LIMIT),
        name="insert",
    )(meta, new, *received)


def emit_kernel(new, f, g, new_out, f_out, g_out, sem):
    ends = ((new, new_out), (f, f_out), (g, g_out))
    copies = [pltpu.make_async_copy(*pair, sem.at[n]) for n, pair in enumerate(ends)]
    for copy in copies:
        copy.start()
    for copy in copies:
        copy.wait()


def emit(new, f, g):
    box = jax.ShapeDtypeStruct((2, FINE, PLANE), F32)
    return pl.pallas_call(
        emit_kernel,
        out_shape=(jax.ShapeDtypeStruct(BLOCK, F32), box, box),
        in_specs=[VMEM] * 3,
        out_specs=[HBM] * 3,
        scratch_shapes=[pltpu.SemaphoreType.DMA((3,))],
        compiler_params=pltpu.CompilerParams(vmem_limit_bytes=LIMIT),
        cost_estimate=pl.CostEstimate(flops=0, bytes_accessed=9000000, transcendentals=0),
        name="emit",
    )(new, f, g)


def finish_kernel(meta, new, written, r0, r1, r2, r3, out, got, boxes, sem):
    def region(k):
        return pl.ds(meta[4 + k], BC), pl.ds(pl.multiple_of(meta[8 + k], 16), BC)

    def store(k):
        x, y = region(k)
        return pltpu.make_async_copy(boxes.at[k], out.at[x, y, :], sem.at[k])

    slots = []
    for k in range(MOST):
        slot = k
        for n in reversed(range(k)):
            same = (meta[4 + n] == meta[4 + k]) & (meta[8 + n] == meta[8 + k]) & (meta[n] >= 0)
            slot = jnp.where(same, n, slot)
        slots.append(slot)
    for n, ref in enumerate((r0, r1, r2, r3)):
        got[2 * n : 2 * n + 2] = ref[...]
    lane = lax.broadcasted_iota(jnp.int32, (BC, BC, NZ), 2)
    iotas = box_iotas()
    for k in range(MOST):

        @pl.when(meta[k] >= 0)
        def _():
            slot = slots[k]

            @pl.when(slot == k)
            def _():
                x, y = region(k)
                boxes[k] = new[x, y, :]

            moved = moved_box(meta, got, k, *iotas)
            oz = meta[12 + k]
            boxes[slot] = jnp.where((lane >= oz) & (lane < oz + BC), moved, boxes[slot])

    for k in range(MOST):

        @pl.when((meta[k] >= 0) & (slots[k] == k))
        def _():
            store(k).start()

    for k in range(MOST):

        @pl.when((meta[k] >= 0) & (slots[k] == k))
        def _():
            store(k).wait()


def finish(meta, new, written, received):
    return pl.pallas_call(
        finish_kernel,
        out_shape=jax.ShapeDtypeStruct(BLOCK, F32),
        in_specs=[SMEM, VMEM, ANY] + [VMEM] * 4,
        out_specs=ANY,
        input_output_aliases={2: 0},
        scratch_shapes=[
            pltpu.VMEM((8, BC, BC * BC), F32),
            pltpu.VMEM((MOST, BC, BC, NZ), F32),
            pltpu.SemaphoreType.DMA((MOST,)),
        ],
        compiler_params=pltpu.CompilerParams(vmem_limit_bytes=LIMIT),
        name="finish",
    )(meta, new, written, *received)


def ring(size, by):
    return [(i, (i + by) % size) for i in range(size)]


def halo(meta, xup, xdn, yup, ydn):
    xlo = lax.ppermute(xup, "tile", ring(8, 1))
    xhi = lax.ppermute(xdn, "tile", ring(8, -1))
    yup, ydn = corners(meta, yup, ydn, xlo, xhi)
    ylo = lax.ppermute(yup, "bulk", ring(16, 1))
    yhi = lax.ppermute(ydn, "bulk", ring(16, -1))
    return xlo, xhi, ylo, yhi


def trade(values):
    done = [values[0]]
    for value, away in zip(values[1:], (1, 64, 65)):
        done.append(lax.ppermute(value, ("tile", "bulk"), [(d, d ^ away) for d in range(128)]))
    return done


def on_device(
    coarse_now,
    coarse_before,
    coarse_courant,
    coarse_absorb,
    fine_now,
    fine_before,
    fine_courant,
    fine_absorb,
    box_anchor,
    intersection,
):
    place = jnp.stack([lax.axis_index("tile"), lax.axis_index("bulk")]).astype(jnp.int32)
    meta = jnp.concatenate([intersection.reshape(16), box_anchor.reshape(6), place])
    consts = tables()
    inputs = (coarse_now, coarse_before, coarse_courant, coarse_absorb)
    extras = halo(meta, *x_edges(*inputs), *y_edges(*inputs))
    weights = factors(fine_courant, fine_absorb)
    first = ahead(fine_now, fine_before, weights, consts[0])
    raw, two, side, start = first_inner(*inputs)
    new, *faces = coarse(True, meta, start, raw, side, extras, extras)
    f, g, res = fine(meta, fine_now, first, weights, trade(faces), consts)
    middle, *packed = insert(meta, new, trade([res] * 4))
    first = ahead(f, g, weights, consts[0])
    halos = halo(meta, *packed)
    raw, q = second_inner(middle, start, two, side)
    new, *faces = coarse(False, meta, middle, raw, side, halos, extras)
    f, g, res = fine(meta, f, first, weights, trade(faces), consts)
    written, f, g = emit(new, f, g)
    p = finish(meta, new, written, trade([res] * 4))
    return p, q, f, g


def solution(mesh):
    grid = P("tile", "bulk", None)
    boxes = P(("tile", "bulk"), None, None)
    in_specs = (grid,) * 4 + (boxes,) * 4 + (P(("tile", "bulk"), None), boxes)
    return jax.shard_map(
        on_device, mesh=mesh, in_specs=in_specs, out_specs=(grid, grid, boxes, boxes), check_vma=False
    )
```

```python
import functools

import jax
import jax.numpy as jnp
import numpy as np
from jax import lax
from jax.experimental import pallas as pl
from jax.experimental.pallas import tpu as pltpu
from jax.sharding import PartitionSpec as P

CX = 64
CY = 64
NZ = 128
BC = 16
FINE = 48
PLANE = FINE * FINE
MOST = 4
F32 = jnp.float32
BF16 = jnp.bfloat16
ANY = pl.BlockSpec(memory_space=pl.ANY)
HBM = pl.BlockSpec(memory_space=pltpu.HBM)
VMEM = pl.BlockSpec(memory_space=pltpu.VMEM)
SMEM = pl.BlockSpec(memory_space=pltpu.SMEM)
LIMIT = 20 * 1024 * 1024


def tables():
    flat = np.arange(PLANE)
    y, z = flat // FINE, flat % FINE
    masks = np.stack([z > 0, z < FINE - 1]).astype(np.float32)
    masks = np.repeat(masks[:, None, :384], 8, axis=1)
    r = np.arange(BC)[:, None]
    spread = np.zeros((128, PLANE), np.float32)
    spread[0:16] = (y == 0) & (z // 3 == r)
    spread[16:32] = (y == FINE - 1) & (z // 3 == r)
    spread[32:48] = (z == 0) & (y // 3 == r)
    spread[48:64] = (z == FINE - 1) & (y // 3 == r)
    spread[64:80] = z // 3 == r
    spread[80:96] = z // 3 == r
    spread = np.concatenate([spread, spread], axis=0)
    pick = (y // 3 == r).astype(np.float32)
    pool = ((y // 3 * BC + z // 3)[:, None] == np.arange(BC * BC)[None, :]).astype(np.float32)
    return jnp.asarray(masks), jnp.asarray(spread, BF16), jnp.asarray(pick), jnp.asarray(pool, BF16)


def partner_of(meta, device):
    away = (meta[22] * 16 + meta[23]) ^ device
    return (away & 1) + 2 * ((away >> 6) & 1)


def far(value):
    return pltpu.with_memory_space_constraint(value, pltpu.HBM)


def split(value):
    high = value.astype(BF16)
    low = (value - high.astype(F32)).astype(BF16)
    return high, low


def dot(left, right):
    return jnp.dot(left, right, preferred_element_type=F32)


def x_edges_kernel(p, q, c, a, xup, xdn, sem):
    ends = [(p.at[CX - 2 : CX], xup.at[0:2]), (p.at[0:2], xdn.at[0:2])]
    for n, ref in enumerate((q, c, a)):
        ends.append((ref.at[CX - 1], xup.at[n + 2]))
        ends.append((ref.at[0], xdn.at[n + 2]))
    copies = [pltpu.make_async_copy(*pair, sem.at[n]) for n, pair in enumerate(ends)]
    for copy in copies:
        copy.start()
    for copy in copies:
        copy.wait()


def x_edges(p, q, c, a):
    x = jax.ShapeDtypeStruct((5, CY, NZ), F32)
    return pl.pallas_call(
        x_edges_kernel,
        out_shape=(x, x),
        in_specs=[HBM] * 4,
        out_specs=[VMEM] * 2,
        scratch_shapes=[pltpu.SemaphoreType.DMA((8,))],
        compiler_params=pltpu.CompilerParams(vmem_limit_bytes=LIMIT),
        name="x_edges",
    )(*[far(v) for v in (p, q, c, a)])


def y_edges_kernel(p, q, c, a, yup, ydn, tiles, sem):
    ends = []
    for n, ref in enumerate((p, q, c, a)):
        ends.append((ref.at[:, CY - 8 : CY, :], tiles.at[0, n]))
        ends.append((ref.at[:, 0:8, :], tiles.at[1, n]))
    copies = [pltpu.make_async_copy(*pair, sem.at[n]) for n, pair in enumerate(ends)]
    for copy in copies:
        copy.start()
    for copy in copies:
        copy.wait()

    def plane(side, n, y):
        return tiles.at[side, n].reshape(CX * 8, NZ)[pl.ds(y, CX, stride=8), :]

    yup[0:64, :] = plane(0, 0, 6)
    yup[64:128, :] = plane(0, 0, 7)
    ydn[0:64, :] = plane(1, 0, 0)
    ydn[64:128, :] = plane(1, 0, 1)
    for n in range(1, 4):
        yup[64 * (n + 1) : 64 * (n + 2), :] = plane(0, n, 7)
        ydn[64 * (n + 1) : 64 * (n + 2), :] = plane(1, n, 0)
    yup[320:328, :] = jnp.zeros((8, NZ), F32)
    ydn[320:328, :] = jnp.zeros((8, NZ), F32)


def y_edges(p, q, c, a):
    y = jax.ShapeDtypeStruct((5 * CX + 8, NZ), F32)
    return pl.pallas_call(
        y_edges_kernel,
        out_shape=(y, y),
        in_specs=[HBM] * 4,
        out_specs=[VMEM] * 2,
        scratch_shapes=[pltpu.VMEM((2, 4, CX, 8, NZ), F32), pltpu.SemaphoreType.DMA((8,))],
        compiler_params=pltpu.CompilerParams(vmem_limit_bytes=LIMIT),
        cost_estimate=pl.CostEstimate(flops=0, bytes_accessed=5000000, transcendentals=0),
        name="y_edges",
    )(*[far(v) for v in (p, q, c, a)])


def corners_kernel(base, meta, yup, ydn, xlo, xhi, yup_out, ydn_out, rows, sem):
    lo = meta[22] > 0
    hi = meta[22] < 7
    for n, y in ((0, CY - 1), (1, 0)):
        rows[n, 0:1, :] = jnp.where(lo, xlo[1, y : y + 1, :], 0.0)
        rows[n, 1:2, :] = jnp.where(hi, xhi[0, y : y + 1, :], 0.0)
    copies = [
        pltpu.make_async_copy(rows.at[0], yup_out.at[base : base + 8, :], sem.at[0]),
        pltpu.make_async_copy(rows.at[1], ydn_out.at[base : base + 8, :], sem.at[1]),
    ]
    for copy in copies:
        copy.start()
    for copy in copies:
        copy.wait()


def corners(meta, yup, ydn, xlo, xhi):
    base = yup.shape[0] - 8
    y = jax.ShapeDtypeStruct(yup.shape, F32)
    return pl.pallas_call(
        functools.partial(corners_kernel, base),
        out_shape=(y, y),
        in_specs=[SMEM, ANY, ANY, VMEM, VMEM],
        out_specs=[ANY, ANY],
        input_output_aliases={1: 0, 2: 1},
        scratch_shapes=[pltpu.VMEM((2, 8, NZ), F32), pltpu.SemaphoreType.DMA((2,))],
        compiler_params=pltpu.CompilerParams(vmem_limit_bytes=LIMIT),
        name="corners",
    )(meta, yup, ydn, xlo, xhi)


def inverse(value):
    guess = pl.reciprocal(value, approx=True)
    guess = guess * (2.0 - value * guess)
    return guess * (2.0 - value * guess)


def lanes_both_ways(here):
    lane = lax.broadcasted_iota(jnp.int32, here.shape, 1)
    before = jnp.where(lane > 0, pltpu.roll(here, 1, 1), 0.0)
    after = jnp.where(lane < NZ - 1, pltpu.roll(here, NZ - 1, 1), 0.0)
    return before + after


def advance(here, beside, before, courant, absorb):
    inv = inverse(1.0 + absorb)
    return before + (2.0 * inv) * (here - before) + (courant * inv) * (beside - 6.0 * here)


CHUNKS = 4
ROWS = CX // CHUNKS
BLOCK = (CX, CY, NZ)
PADDED = (CX + 2, CY + 16, NZ)


def clear_rim(pe):
    edge = jnp.zeros((CX, 8, NZ), F32)
    pe[1 : CX + 1, 0:8, :] = edge
    pe[1 : CX + 1, CY + 8 : CY + 16, :] = edge
    pe[0] = jnp.zeros((CY + 16, NZ), F32)
    pe[CX + 1] = jnp.zeros((CY + 16, NZ), F32)


def around(pe, x):
    here = pe[x + 1, 8 : CY + 8, :]
    beside = pe[x, 8 : CY + 8, :] + pe[x + 2, 8 : CY + 8, :]
    beside = beside + pe[x + 1, 7 : CY + 7, :] + pe[x + 1, 9 : CY + 9, :]
    return here, beside + lanes_both_ways(here)


def first_inner_kernel(p, q, c, a, raw, two, side, here_out, pe, qs, cs, as_, sem):
    copies = []
    for n in range(CHUNKS):
        s = slice(ROWS * n, ROWS * n + ROWS)
        to_rows = slice(1 + ROWS * n, 1 + ROWS * n + ROWS)
        part = [pltpu.make_async_copy(p.at[s], pe.at[to_rows, 8 : CY + 8, :], sem.at[0, n])]
        for m, (ref, to) in enumerate(((q, qs), (c, cs), (a, as_))):
            part.append(pltpu.make_async_copy(ref.at[s], to.at[s], sem.at[m + 1, n]))
        copies.append(part)
    for part in copies:
        for copy in part:
            copy.start()
    clear_rim(pe)
    copies[0][0].wait()

    def body(x, carry):
        here, beside = around(pe, x)
        inv = inverse(1.0 + as_[x])
        twice = 2.0 * inv
        weight = cs[x] * inv
        two[x] = twice
        side[x] = weight
        here_out[x] = here
        raw[x] = qs[x] + twice * (here - qs[x]) + weight * (beside - 6.0 * here)
        return carry

    for n in range(CHUNKS):
        if n + 1 < CHUNKS:
            copies[n + 1][0].wait()
        for copy in copies[n][1:]:
            copy.wait()
        lax.fori_loop(ROWS * n, ROWS * n + ROWS, body, 0, unroll=8)


def first_inner(p, q, c, a):
    block = jax.ShapeDtypeStruct(BLOCK, F32)
    return pl.pallas_call(
        first_inner_kernel,
        out_shape=(block, block, block, block),
        in_specs=[HBM] * 4,
        out_specs=[VMEM] * 4,
        scratch_shapes=[
            pltpu.VMEM(PADDED, F32),
            pltpu.VMEM(BLOCK, F32),
            pltpu.VMEM(BLOCK, F32),
            pltpu.VMEM(BLOCK, F32),
            pltpu.SemaphoreType.DMA((4, CHUNKS)),
        ],
        compiler_params=pltpu.CompilerParams(vmem_limit_bytes=LIMIT),
        cost_estimate=pl.CostEstimate(flops=12000000, bytes_accessed=10000000, transcendentals=0),
        name="first_inner",
    )(*[far(v) for v in (p, q, c, a)])


def second_inner_kernel(p, q, two, side, raw, out, pe, sem):
    store = pltpu.make_async_copy(p, out, sem)
    store.start()
    clear_rim(pe)

    def fill(x, carry):
        pe[x + 1, 8 : CY + 8, :] = p[x]
        return carry

    lax.fori_loop(0, CX, fill, 0, unroll=8)

    def body(x, carry):
        here, beside = around(pe, x)
        raw[x] = q[x] + two[x] * (here - q[x]) + side[x] * (beside - 6.0 * here)
        return carry

    lax.fori_loop(0, CX, body, 0, unroll=8)
    store.wait()


def second_inner(p, q, two, side):
    return pl.pallas_call(
        second_inner_kernel,
        out_shape=(jax.ShapeDtypeStruct(BLOCK, F32),) * 2,
        in_specs=[VMEM] * 4,
        out_specs=[VMEM, ANY],
        scratch_shapes=[pltpu.VMEM(PADDED, F32), pltpu.SemaphoreType.DMA],
        compiler_params=pltpu.CompilerParams(vmem_limit_bytes=LIMIT),
        cost_estimate=pl.CostEstimate(flops=12000000, bytes_accessed=8000000, transcendentals=0),
        name="second_inner",
    )(p, q, two, side)


def coarse_kernel(
    first,
    meta,
    p,
    raw,
    weight,
    pxlo,
    pxhi,
    pylo,
    pyhi,
    exlo,
    exhi,
    eylo,
    eyhi,
    new,
    face0,
    face1,
    face2,
    face3,
    rim,
    ring,
    faces,
):
    tile, bulk = meta[22], meta[23]
    inside_grid = (tile > 0, tile < 7, bulk > 0, bulk < 15)
    base = pylo.shape[0] - 8
    qlo, qhi = (2, 2) if first else (1, 0)

    def keep(n, value):
        return jnp.where(inside_grid[n], value, 0.0)

    def body(x, carry):
        new[x] = raw[x]
        return carry

    lax.fori_loop(0, CX, body, 0, unroll=8)

    def plane(ref, y):
        return ref.reshape(CX * CY, NZ)[pl.ds(y, CX, stride=CY), :]

    def corner(n, ref, at):
        return keep(n, ref[base + at : base + at + 1, :])

    def extra(ref, n):
        return ref[n] if len(ref.shape) == 3 else ref[64 * n : 64 * n + 64, :]

    sides = (
        (pxlo[1], pxlo[0], p[0], corner(2, pylo, 0), corner(3, pyhi, 0), exlo, qlo),
        (pxhi[0], pxhi[1], p[CX - 1], corner(2, pylo, 1), corner(3, pyhi, 1), exhi, qhi),
        (pylo[64:128, :], pylo[0:64, :], plane(p, 0), *[pylo[base + n : base + n + 1, :] for n in (0, 1)], eylo, qlo),
        (pyhi[0:64, :], pyhi[64:128, :], plane(p, CY - 1), *[pyhi[base + n : base + n + 1, :] for n in (0, 1)], eyhi, qhi),
    )
    for n, (here, out, inside, before, after, ref, at_q) in enumerate(sides):
        here = keep(n, here)
        rim[0, n] = here
        ring[n, 7:8, :] = keep(n, before)
        ring[n, 8:72, :] = here
        ring[n, 72:73, :] = keep(n, after)
        beside = ring[n, 7:71, :] + ring[n, 9:73, :] + keep(n, out) + inside + lanes_both_ways(here)
        rim[1, n] = advance(here, beside, *[keep(n, extra(ref, m)) for m in (at_q, 3, 4)])

    new[0] = new[0] + weight[0] * rim[0, 0]
    new[CX - 1] = new[CX - 1] + weight[CX - 1] * rim[0, 1]
    low = (plane(weight, 0) * rim[0, 2])[:, None, :]
    new[:, 0:1, :] = new[:, 0:1, :] + low
    high = (plane(weight, CY - 1) * rim[0, 3])[:, None, :]
    new[:, CY - 1 : CY, :] = new[:, CY - 1 : CY, :] + high

    from_z = lax.broadcasted_iota(jnp.int32, (NZ, NZ), 0)
    to_lane = lax.broadcasted_iota(jnp.int32, (NZ, NZ), 1)
    out_lane = lax.broadcasted_iota(jnp.int32, (BC, NZ), 1)
    deep_lane = lax.broadcasted_iota(jnp.int32, (BC, BC, NZ), 2)
    deep_y = lax.broadcasted_iota(jnp.int32, (BC, BC, NZ), 1)
    diagonal = (deep_lane & 15) == deep_y

    def entry(k, carry):
        ident = meta[k]

        @pl.when(ident >= 0)
        def _():
            ox = pl.multiple_of(meta[4 + k], 16)
            oy = pl.multiple_of(meta[8 + k], 16)
            oz = meta[12 + k]
            where_to = partner_of(meta, ident >> 1) * 2 + (ident & 1)
            low_face = (to_lane >= 32) & (to_lane < 48)
            high_face = (to_lane >= 48) & (to_lane < 64)
            source = jnp.where(
                low_face, oz - 1, jnp.where(high_face, oz + BC, oz + (to_lane & 15))
            )
            mover = jnp.where(from_z == source, 1.0, 0.0).astype(BF16)
            mover = jnp.concatenate([mover, mover], axis=0)
            for t, ref in enumerate((p, new)):
                cube = ref[pl.ds(ox, BC), pl.ds(oy, BC), :].reshape(BC * BC, NZ)
                y = pl.multiple_of(jnp.maximum(oy - 8, 0), 8)
                ym = ref[pl.ds(ox, BC), pl.ds(y, 8), :][:, 7, :]
                ym = jnp.where(oy == 0, rim[t, 2, pl.ds(ox, BC), :], ym)
                y = pl.multiple_of(jnp.minimum(oy + BC, CY - 8), 8)
                yp = ref[pl.ds(ox, BC), pl.ds(y, 8), :][:, 0, :]
                yp = jnp.where(oy == CY - BC, rim[t, 3, pl.ds(ox, BC), :], yp)
                xm = ref[jnp.maximum(ox - 1, 0), pl.ds(oy, BC), :]
                xm = jnp.where(ox == 0, rim[t, 0, pl.ds(oy, BC), :], xm)
                xp = ref[jnp.minimum(ox + BC, CX - 1), pl.ds(oy, BC), :]
                xp = jnp.where(ox == CX - BC, rim[t, 1, pl.ds(oy, BC), :], xp)
                high, low = split(jnp.concatenate([cube, ym, yp, xm, xp], axis=0))
                moved = dot(jnp.concatenate([high, low], axis=1), mover)
                z_face = jnp.where(diagonal, moved[0:256].reshape(BC, BC, NZ), 0.0).sum(axis=1)
                tile_ = jnp.where(out_lane < 80, moved[288:304], moved[304:320])
                tile_ = jnp.where(out_lane < 64, z_face, tile_)
                tile_ = jnp.where(out_lane < 32, moved[272:288], tile_)
                tile_ = jnp.where(out_lane < 16, moved[256:272], tile_)
                faces[where_to, t] = tile_

        return carry

    lax.fori_loop(0, MOST, entry, 0)
    for n, ref in enumerate((face0, face1, face2, face3)):
        ref[...] = faces[2 * n : 2 * n + 2]


def coarse(first, meta, p, raw, weight, halos, extras):
    face = jax.ShapeDtypeStruct((2, 2, BC, NZ), F32)
    return pl.pallas_call(
        functools.partial(coarse_kernel, first),
        out_shape=(jax.ShapeDtypeStruct(BLOCK, F32), face, face, face, face),
        in_specs=[SMEM] + [VMEM] * 11,
        out_specs=[VMEM] * 5,
        scratch_shapes=[
            pltpu.VMEM((2, 4, 64, NZ), F32),
            pltpu.VMEM((4, 80, NZ), F32),
            pltpu.VMEM((8, 2, BC, NZ), F32),
        ],
        compiler_params=pltpu.CompilerParams(vmem_limit_bytes=LIMIT),
        name="coarse",
    )(meta, p, raw, weight, *halos, *extras)


def factors_kernel(c, a, one, two, three, cs, as_, sem):
    copies = []
    for j in range(2):
        copies.append(pltpu.make_async_copy(c.at[j], cs.at[j], sem.at[2 * j]))
        copies.append(pltpu.make_async_copy(a.at[j], as_.at[j], sem.at[2 * j + 1]))
    for copy in copies:
        copy.start()
    for j in range(2):
        copies[2 * j].wait()
        copies[2 * j + 1].wait()

        def body(i, carry):
            s = pl.ds(pl.multiple_of(8 * i, 8), 8)
            inv = inverse(1.0 + as_[j, s, :])
            side = cs[j, s, :] * inv
            three[j, s, :] = side
            one[j, s, :] = 2.0 * inv - 6.0 * side
            two[j, s, :] = 1.0 - 2.0 * inv
            return carry

        lax.fori_loop(0, FINE // 8, body, 0, unroll=2)


def factors(c, a):
    box = jax.ShapeDtypeStruct((2, FINE, PLANE), F32)
    return pl.pallas_call(
        factors_kernel,
        out_shape=(box, box, box),
        in_specs=[HBM] * 2,
        out_specs=[VMEM] * 3,
        scratch_shapes=[pltpu.VMEM(box.shape, F32)] * 2 + [pltpu.SemaphoreType.DMA((4,))],
        compiler_params=pltpu.CompilerParams(vmem_limit_bytes=LIMIT),
        cost_estimate=pl.CostEstimate(flops=3000000, bytes_accessed=4000000, transcendentals=0),
        name="factors",
    )(far(c), far(a))


def turned(v):
    return {d: (pltpu.roll(v, d, 1), pltpu.roll(v, 128 - d, 1)) for d in (1, 48)}


def beside_in_plane(row, masks):
    small = lax.broadcasted_iota(jnp.int32, (8, 128), 1)
    zero = jnp.zeros((8, 128), F32)
    none = {d: (zero, zero) for d in (1, 48)}
    cur = row(0)
    cur_t = turned(cur)
    before_t = none
    masks = [[masks[n, :, 128 * r : 128 * r + 128] for r in range(3)] for n in range(2)]
    for k in range(PLANE // 128):
        ls = slice(128 * k, 128 * k + 128)
        last = k + 1 == PLANE // 128
        nxt = cur if last else row(k + 1)
        nxt_t = none if last else turned(nxt)
        total = jnp.where(small < 48, before_t[48][0], cur_t[48][0])
        total = total + jnp.where(small >= 80, nxt_t[48][1], cur_t[48][1])
        down = jnp.where(small < 1, before_t[1][0], cur_t[1][0])
        up = jnp.where(small >= 127, nxt_t[1][1], cur_t[1][1])
        total = total + down * masks[0][k % 3] + up * masks[1][k % 3]
        yield ls, cur, total
        before_t, cur, cur_t = cur_t, nxt, nxt_t


def ahead_kernel(f, g, one, two, three, masks, raw, buf, sem):
    copies = [pltpu.make_async_copy(f.at[j], buf.at[j, 8:56, :], sem.at[j]) for j in range(2)]
    for copy in copies:
        copy.start()
    for j in range(2):
        buf[j, 0:8, :] = jnp.zeros((8, PLANE), F32)
        buf[j, 56:64, :] = jnp.zeros((8, PLANE), F32)
    for copy in copies:
        copy.wait()

    def box(j, carry):
        for i in range(6):
            s = slice(8 * i, 8 * i + 8)

            def row(k):
                return buf[j, 8 + 8 * i : 16 + 8 * i, 128 * k : 128 * k + 128]

            for ls, cur, total in beside_in_plane(row, masks):
                total = total + buf[j, 7 + 8 * i : 15 + 8 * i, ls] + buf[j, 9 + 8 * i : 17 + 8 * i, ls]
                raw[j, s, ls] = (
                    one[j, s, ls] * cur + two[j, s, ls] * g[j, s, ls] + three[j, s, ls] * total
                )
        return carry

    lax.fori_loop(0, 2, box, 0, unroll=True)


def ahead(f, g, weights, masks):
    box = jax.ShapeDtypeStruct((2, FINE, PLANE), F32)
    return pl.pallas_call(
        ahead_kernel,
        out_shape=box,
        in_specs=[ANY] + [VMEM] * 5,
        out_specs=VMEM,
        scratch_shapes=[pltpu.VMEM((2, 64, PLANE), F32), pltpu.SemaphoreType.DMA((2,))],
        compiler_params=pltpu.CompilerParams(vmem_limit_bytes=LIMIT),
        cost_estimate=pl.CostEstimate(flops=5000000, bytes_accessed=5000000, transcendentals=0),
        name="ahead",
    )(f, g, *weights, masks)


def fine_kernel(
    meta,
    f,
    raw,
    one,
    two,
    three,
    r0,
    r1,
    r2,
    r3,
    masks,
    spread,
    pick,
    pool,
    f_out,
    g_out,
    res,
    buf,
    ghost,
    xrow,
    faces,
):
    for n, ref in enumerate((r0, r1, r2, r3)):
        faces[2 * n : 2 * n + 2] = ref[...]

    lane = lax.broadcasted_iota(jnp.int32, (BC, NZ), 1)
    wide_lane = jnp.concatenate([lane, lane], axis=1)
    tall = lax.broadcasted_iota(jnp.int32, (FINE, BC), 0)
    wide = lax.broadcasted_iota(jnp.int32, (FINE, BC), 1)
    thrice = jnp.where((tall >= 3 * wide) & (tall < 3 * wide + 3), 1.0, 0.0).astype(BF16)
    sides, rows = [], []
    for j in range(2):
        source = (meta[16 + 3 * j] >> 6) * 16 + (meta[17 + 3 * j] >> 6)
        at = partner_of(meta, source) * 2 + j
        old = jnp.where(lane < 96, faces[at, 0], 0.0)
        new = jnp.where(lane < 96, faces[at, 1], 0.0)
        for m in range(3):
            high, low = split(old + (m / 3.0) * (new - old))
            both = jnp.concatenate([high, low], axis=1)
            zero = jnp.zeros_like(both)
            sides.append(jnp.where(wide_lane < 64, both, zero))
            rows.append(jnp.where((wide_lane >= 64) & (wide_lane < 80), both, zero))
            rows.append(jnp.where(wide_lane >= 80, both, zero))
    tall_sides = dot(thrice, jnp.concatenate(sides, axis=1)).astype(BF16)
    sides = [tall_sides[:, 256 * n : 256 * n + 256] for n in range(6)]
    spreaded = dot(jnp.concatenate(sides + rows, axis=0), spread[...])
    for j in range(2):
        for m in range(3):
            at = 48 * (3 * j + m)
            ghost[m, j] = spreaded[at : at + 48]
        for n in range(6):
            at = 288 + 16 * (6 * j + n)
            part = spreaded[at : at + 16] * pick[...]
            xrow[j, n : n + 1, :] = part.sum(axis=0, keepdims=True)

    def first(j):
        for i in range(6):
            s = slice(8 * i, 8 * i + 8)
            buf[0, j, 8 + 8 * i : 16 + 8 * i, :] = raw[j, s, :] + three[j, s, :] * ghost[0, j, s, :]
        for n, x in ((0, 0), (1, FINE - 1)):
            buf[0, j, 8 + x : 9 + x, :] = (
                buf[0, j, 8 + x : 9 + x, :] + three[j, x : x + 1, :] * xrow[j, n : n + 1, :]
            )

    def substep(m, j):
        buf[m - 1, j, 7:8, :] = xrow[j, 2 * m : 2 * m + 1, :]
        buf[m - 1, j, 56:57, :] = xrow[j, 2 * m + 1 : 2 * m + 2, :]
        for i in range(6):
            s = slice(8 * i, 8 * i + 8)
            pad = slice(8 + 8 * i, 16 + 8 * i)

            def row(k):
                return buf[m - 1, j, pad, 128 * k : 128 * k + 128]

            for ls, cur, total in beside_in_plane(row, masks):
                total = total + ghost[m, j, s, ls]
                total = total + (
                    buf[m - 1, j, 7 + 8 * i : 15 + 8 * i, ls]
                    + buf[m - 1, j, 9 + 8 * i : 17 + 8 * i, ls]
                )
                old = f[j, s, ls] if m == 1 else buf[0, j, pad, ls]
                value = one[j, s, ls] * cur + two[j, s, ls] * old + three[j, s, ls] * total
                if m == 1:
                    buf[1, j, pad, ls] = value
                    g_out[j, s, ls] = value
                else:
                    f_out[j, s, ls] = value

    def box(j, carry):
        first(j)
        substep(1, j)
        substep(2, j)
        return carry

    lax.fori_loop(0, 2, box, 0, unroll=True)
    tall = lax.broadcasted_iota(jnp.int32, (BC, FINE), 1)
    wide = lax.broadcasted_iota(jnp.int32, (BC, FINE), 0)
    gather = jnp.where((tall >= 3 * wide) & (tall < 3 * wide + 3), 1.0, 0.0).astype(BF16)
    parts = [part for j in range(2) for part in split(f_out[j])]
    pooled = dot(jnp.concatenate(parts, axis=0), pool[...])
    parts = []
    for j in range(2):
        parts += split(pooled[96 * j : 96 * j + 48] + pooled[96 * j + 48 : 96 * j + 96])
    means = dot(gather, jnp.concatenate(parts, axis=1))
    for j in range(2):
        at = 512 * j
        res[j] = (means[:, at : at + 256] + means[:, at + 256 : at + 512]) * (1.0 / 27.0)


def fine(meta, f, raw, weights, received, consts):
    box = jax.ShapeDtypeStruct((2, FINE, PLANE), F32)
    return pl.pallas_call(
        fine_kernel,
        out_shape=(box, box, jax.ShapeDtypeStruct((2, BC, BC * BC), F32)),
        in_specs=[SMEM] + [VMEM] * 13,
        out_specs=[VMEM] * 3,
        scratch_shapes=[
            pltpu.VMEM((2, 2, 64, PLANE), F32),
            pltpu.VMEM((3, 2, FINE, PLANE), F32),
            pltpu.VMEM((2, 8, PLANE), F32),
            pltpu.VMEM((8, 2, BC, NZ), F32),
        ],
        compiler_params=pltpu.CompilerParams(vmem_limit_bytes=LIMIT),
        name="fine",
    )(meta, f, raw, *weights, *received, *consts)


def moved_box(meta, got, k, mine, from_yz, to_lane):
    ident = meta[k]
    value = got[partner_of(meta, ident >> 1) * 2 + (ident & 1)]
    full = jnp.where(mine, value[:, None, :], 0.0).reshape(BC * BC, BC * BC)
    high, low = split(full)
    mover = jnp.where(to_lane == meta[12 + k] + (from_yz & 15), 1.0, 0.0).astype(BF16)
    moved = dot(jnp.concatenate([high, low], axis=1), jnp.concatenate([mover, mover], axis=0))
    return moved.reshape(BC, BC, NZ)


def box_iotas():
    y_of = lax.broadcasted_iota(jnp.int32, (BC, BC, BC * BC), 1)
    lane_of = lax.broadcasted_iota(jnp.int32, (BC, BC, BC * BC), 2)
    from_yz = lax.broadcasted_iota(jnp.int32, (BC * BC, NZ), 0)
    to_lane = lax.broadcasted_iota(jnp.int32, (BC * BC, NZ), 1)
    return (lane_of >> 4) == y_of, from_yz, to_lane


def insert_kernel(meta, new, r0, r1, r2, r3, out, xup, xdn, yup, ydn, got):
    for n, ref in enumerate((r0, r1, r2, r3)):
        got[2 * n : 2 * n + 2] = ref[...]

    def body(x, carry):
        out[x] = new[x]
        return carry

    lax.fori_loop(0, CX, body, 0, unroll=8)
    lane = lax.broadcasted_iota(jnp.int32, (BC, BC, NZ), 2)
    iotas = box_iotas()

    def entry(k, carry):
        @pl.when(meta[k] >= 0)
        def _():
            at = (pl.ds(meta[4 + k], BC), pl.ds(pl.multiple_of(meta[8 + k], 16), BC))
            moved = moved_box(meta, got, k, *iotas)
            oz = meta[12 + k]
            out[at[0], at[1], :] = jnp.where(
                (lane >= oz) & (lane < oz + BC), moved, out[at[0], at[1], :]
            )

        return carry

    lax.fori_loop(0, MOST, entry, 0)

    def plane(y):
        return out.reshape(CX * CY, NZ)[pl.ds(y, CX, stride=CY), :]

    xup[...] = out[CX - 2 : CX]
    xdn[...] = out[0:2]
    yup[0:64, :] = plane(CY - 2)
    yup[64:128, :] = plane(CY - 1)
    ydn[0:64, :] = plane(0)
    ydn[64:128, :] = plane(1)
    yup[128:136, :] = jnp.zeros((8, NZ), F32)
    ydn[128:136, :] = jnp.zeros((8, NZ), F32)


def insert(meta, new, received):
    x = jax.ShapeDtypeStruct((2, CY, NZ), F32)
    y = jax.ShapeDtypeStruct((2 * CX + 8, NZ), F32)
    return pl.pallas_call(
        insert_kernel,
        out_shape=(jax.ShapeDtypeStruct(BLOCK, F32), x, x, y, y),
        in_specs=[SMEM] + [VMEM] * 5,
        out_specs=[VMEM] * 5,
        scratch_shapes=[pltpu.VMEM((8, BC, BC * BC), F32)],
        compiler_params=pltpu.CompilerParams(vmem_limit_bytes=LIMIT),
        name="insert",
    )(meta, new, *received)


def emit_kernel(new, f, g, new_out, f_out, g_out, sem):
    ends = ((new, new_out), (f, f_out), (g, g_out))
    copies = [pltpu.make_async_copy(*pair, sem.at[n]) for n, pair in enumerate(ends)]
    for copy in copies:
        copy.start()
    for copy in copies:
        copy.wait()


def emit(new, f, g):
    box = jax.ShapeDtypeStruct((2, FINE, PLANE), F32)
    return pl.pallas_call(
        emit_kernel,
        out_shape=(jax.ShapeDtypeStruct(BLOCK, F32), box, box),
        in_specs=[VMEM] * 3,
        out_specs=[HBM] * 3,
        scratch_shapes=[pltpu.SemaphoreType.DMA((3,))],
        compiler_params=pltpu.CompilerParams(vmem_limit_bytes=LIMIT),
        cost_estimate=pl.CostEstimate(flops=0, bytes_accessed=9000000, transcendentals=0),
        name="emit",
    )(new, f, g)


def finish_kernel(meta, new, written, r0, r1, r2, r3, out, got, boxes, sem):
    def region(k):
        return pl.ds(meta[4 + k], BC), pl.ds(pl.multiple_of(meta[8 + k], 16), BC)

    def store(k):
        x, y = region(k)
        return pltpu.make_async_copy(boxes.at[k], out.at[x, y, :], sem.at[k])

    slots = []
    for k in range(MOST):
        slot = k
        for n in reversed(range(k)):
            same = (meta[4 + n] == meta[4 + k]) & (meta[8 + n] == meta[8 + k]) & (meta[n] >= 0)
            slot = jnp.where(same, n, slot)
        slots.append(slot)
    for n, ref in enumerate((r0, r1, r2, r3)):
        got[2 * n : 2 * n + 2] = ref[...]
    lane = lax.broadcasted_iota(jnp.int32, (BC, BC, NZ), 2)
    iotas = box_iotas()
    for k in range(MOST):

        @pl.when(meta[k] >= 0)
        def _():
            slot = slots[k]

            @pl.when(slot == k)
            def _():
                x, y = region(k)
                boxes[k] = new[x, y, :]

            moved = moved_box(meta, got, k, *iotas)
            oz = meta[12 + k]
            boxes[slot] = jnp.where((lane >= oz) & (lane < oz + BC), moved, boxes[slot])

    for k in range(MOST):

        @pl.when((meta[k] >= 0) & (slots[k] == k))
        def _():
            store(k).start()

    for k in range(MOST):

        @pl.when((meta[k] >= 0) & (slots[k] == k))
        def _():
            store(k).wait()


def finish(meta, new, written, received):
    return pl.pallas_call(
        finish_kernel,
        out_shape=jax.ShapeDtypeStruct(BLOCK, F32),
        in_specs=[SMEM, VMEM, ANY] + [VMEM] * 4,
        out_specs=ANY,
        input_output_aliases={2: 0},
        scratch_shapes=[
            pltpu.VMEM((8, BC, BC * BC), F32),
            pltpu.VMEM((MOST, BC, BC, NZ), F32),
            pltpu.SemaphoreType.DMA((MOST,)),
        ],
        compiler_params=pltpu.CompilerParams(vmem_limit_bytes=LIMIT),
        name="finish",
    )(meta, new, written, *received)


def ring(size, by):
    return [(i, (i + by) % size) for i in range(size)]


def halo(meta, xup, xdn, yup, ydn):
    xlo = lax.ppermute(xup, "tile", ring(8, 1))
    xhi = lax.ppermute(xdn, "tile", ring(8, -1))
    yup, ydn = corners(meta, yup, ydn, xlo, xhi)
    ylo = lax.ppermute(yup, "bulk", ring(16, 1))
    yhi = lax.ppermute(ydn, "bulk", ring(16, -1))
    return xlo, xhi, ylo, yhi


def trade(values):
    done = [values[0]]
    for value, away in zip(values[1:], (1, 64, 65)):
        done.append(lax.ppermute(value, ("tile", "bulk"), [(d, d ^ away) for d in range(128)]))
    return done


def on_device(
    coarse_now,
    coarse_before,
    coarse_courant,
    coarse_absorb,
    fine_now,
    fine_before,
    fine_courant,
    fine_absorb,
    box_anchor,
    intersection,
):
    place = jnp.stack([lax.axis_index("tile"), lax.axis_index("bulk")]).astype(jnp.int32)
    meta = jnp.concatenate([intersection.reshape(16), box_anchor.reshape(6), place])
    consts = tables()
    inputs = (coarse_now, coarse_before, coarse_courant, coarse_absorb)
    extras = halo(meta, *x_edges(*inputs), *y_edges(*inputs))
    weights = factors(fine_courant, fine_absorb)
    first = ahead(fine_now, fine_before, weights, consts[0])
    raw, two, side, start = first_inner(*inputs)
    new, *faces = coarse(True, meta, start, raw, side, extras, extras)
    f, g, res = fine(meta, fine_now, first, weights, trade(faces), consts)
    middle, *packed = insert(meta, new, trade([res] * 4))
    first = ahead(f, g, weights, consts[0])
    halos = halo(meta, *packed)
    raw, q = second_inner(middle, start, two, side)
    new, *faces = coarse(False, meta, middle, raw, side, halos, extras)
    f, g, res = fine(meta, f, first, weights, trade(faces), consts)
    written, f, g = emit(new, f, g)
    p = finish(meta, new, written, trade([res] * 4))
    return p, q, f, g


def solution(mesh):
    grid = P("tile", "bulk", None)
    boxes = P(("tile", "bulk"), None, None)
    in_specs = (grid,) * 4 + (boxes,) * 4 + (P(("tile", "bulk"), None), boxes)
    return jax.shard_map(
        on_device, mesh=mesh, in_specs=in_specs, out_specs=(grid, grid, boxes, boxes), check_vma=False
    )
```
